32 devices in a mesh: frame: 8 (over y, x, core), row: 4 (over z).
Axes of the slice: x: 2, y: 2, z: 4, core: 2. Of those that a mesh axis runs over, the one named last changes fastest.
Arguments:
- spatial_q: bfloat16 [16, 32, 32, 1152], P('frame', 'row'), may hold values from -10.5 to 10.5
- spatial_k: bfloat16 [16, 32, 32, 1152], P('frame', 'row'), may hold values from -10.5 to 10.5
- spatial_v: bfloat16 [16, 32, 32, 1152], P('frame', 'row'), may hold values from -6 to 6
- residual: bfloat16 [16, 32, 32, 1152], P('frame', 'row'), may hold values from -6 to 6
- neighbour_list: int32 [16, 6], P('row'), may hold values from 0 to 15, as said below
- block_mask: int32 [4, 4], replicated, may hold values from 0 to 1, as said below
- out_weight: bfloat16 [1152, 1152], P('frame'), may hold values from -0.1875 to 0.1875
- qkv_weight: bfloat16 [1152, 3456], P('frame'), may hold values from -1.4799 to 1.4799
- pos_embed: float32 [16, 1152], P('frame'), may hold values from -150.5 to 150.5
- mod_shift: float32 [1152], replicated, may hold values from -2 to 2
- mod_scale: float32 [1152], replicated, may hold values from -2 to 2
Outputs:
- temporal_mix: bfloat16 [16, 32, 32, 1152], P('frame', 'row')
The draws below stay inside these ranges and needn't reach their ends.
Inputs may be any that keep to these rules, and one draw needn't show every extreme that they name: `neighbour_list`: each row holds 6 different tiles of its own clip: slot 0 is the row's own tile; every other lies at most one tile row and at most two tile columns away from it, inside the grid of 16 tiles. `block_mask`: entry (i, j) is 1 where i == j and 0 where j > i.
All inputs are finite; a program needn't handle non-finite values.
Results may differ from the reference program's by a relative error of at most 0.0056.
The reference program's roundings to bfloat16 on the way count: a program that leaves them out, or rounds other values in their place, can miss the bound.
Values may be sent and summed in bfloat16 or wider, within the bound.
A program may use at most 128 MiB of HBM per device.

```python
import math
import jax
import jax.numpy as jnp
from jax import lax

D = 1152
HEADS = 16
TILE = 8
SLOTS = 6
ROWS = 32
COLS = 32
BLOCK = 4
FRAMES = 16
CLIPS = 1
TILES_WIDE = 4
TILES = 16
BLOCKS = 4


def spatial_pair(key):
    full_shape = (FRAMES, CLIPS * ROWS, COLS, D)
    key_q, key_k = jax.random.split(jax.random.fold_in(key, 11))
    queries = jnp.clip(jax.random.normal(key_q, full_shape, jnp.float32), -4.0, 4.0)
    key_draw = jnp.clip(jax.random.normal(key_k, full_shape, jnp.float32), -4.0, 4.0)
    return (queries, key_draw)


def draw_spatial_q(key, part):
    return spatial_pair(key)[0].astype(jnp.bfloat16)


def draw_spatial_k(key, part):
    return spatial_pair(key)[1].astype(jnp.bfloat16)


def draw_qkv_weight(key, part):
    key_w = jax.random.fold_in(key, 23)
    drawn = jnp.clip(jax.random.normal(key_w, (D, 3 * D), jnp.float32), -6.0, 6.0) * D ** (-0.5)
    return drawn.astype(jnp.bfloat16)


def draw_pos_embed(key, part):
    key_a = jax.random.fold_in(jax.random.fold_in(key, 37), 0)
    return jnp.clip(jax.random.normal(key_a, (FRAMES, D), jnp.float32), -4.0, 4.0)


def draw_block_mask(key, part):
    bits = jax.random.randint(jax.random.fold_in(key, 31), (BLOCKS, BLOCKS), 0, 2)
    later = jnp.arange(BLOCKS)[:, None]
    earlier = jnp.arange(BLOCKS)[None, :]
    return jnp.where(later == earlier, 1, jnp.where(later > earlier, bits, 0)).astype(jnp.int32)


def draw_neighbour_list(key, part):
    row_step = jnp.array([-1, -1, -1, -1, -1, 0, 0, 0, 0, 1, 1, 1, 1, 1], jnp.int32)
    col_step = jnp.array([-2, -1, 0, 1, 2, -2, -1, 1, 2, -2, -1, 0, 1, 2], jnp.int32)
    list_rows = jnp.arange(CLIPS * TILES, dtype=jnp.int32)
    tile_row = (list_rows // TILES_WIDE + 1) % (TILES // TILES_WIDE)
    tile_col = list_rows % TILES_WIDE
    tile_ids = tile_row * TILES_WIDE + tile_col
    cand_row = tile_row[:, None] + row_step[None, :]
    cand_col = tile_col[:, None] + col_step[None, :]
    inside = (cand_row >= 0) & (cand_row < TILES // TILES_WIDE) & (cand_col >= 0) & (cand_col < TILES_WIDE)
    scores = jax.random.randint(jax.random.fold_in(key, 41), (CLIPS * TILES, 14), 0, 1 << 20) * 16 + jnp.arange(14, dtype=jnp.int32)[None, :]
    scores = jnp.where(inside, scores, scores + (1 << 26))
    ranking = jnp.argsort(scores, axis=1)[:, :SLOTS - 1]
    chosen = jnp.take_along_axis(cand_row * TILES_WIDE + cand_col, ranking, axis=1)
    return jnp.concatenate([tile_ids[:, None], chosen], axis=1).astype(jnp.int32)


def block_levels(key, shape, cuts, smallest, largest):
    loudness = 1.0
    for axis_at, blocks in cuts:
        draws = jax.random.uniform(jax.random.fold_in(jax.random.fold_in(key, 6), axis_at), (blocks,), jnp.float32, smallest / len(cuts), largest / len(cuts))
        loudness = loudness * jnp.repeat(jnp.exp(draws), shape[axis_at] // blocks).reshape((-1,) + (1,) * (len(shape) - 1 - axis_at))
    return loudness


def gaussian(key, dims, scale, bound, shards=(), kind=jnp.bfloat16):
    values = scale * jax.random.normal(key, dims, jnp.float32)
    if shards:
        values = values * block_levels(key, dims, shards, -0.22, 0.18)
    return jnp.clip(values, -bound, bound).astype(kind)


def setup_inputs(seed: int = 0) -> dict:
    key_list = jax.random.split(jax.random.key(seed), 12)
    spatial_q = draw_spatial_q(jax.random.fold_in(key_list[11], 71), 0)
    spatial_k = draw_spatial_k(jax.random.fold_in(key_list[11], 71), 0)
    spatial_v = gaussian(key_list[2], (FRAMES, CLIPS * ROWS, COLS, D), 1.0, 6.0, ((0, 8), (1, 4)))
    residual = gaussian(key_list[3], (FRAMES, CLIPS * ROWS, COLS, D), 1.0, 6.0, ((0, 8), (1, 4)))
    neighbour_list = draw_neighbour_list(jax.random.fold_in(key_list[11], 71), 0)
    block_mask = draw_block_mask(jax.random.fold_in(key_list[11], 71), 0)
    out_weight = gaussian(key_list[6], (D, D), D ** -0.5, 0.1875, ((0, 8),))
    qkv_weight = draw_qkv_weight(jax.random.fold_in(key_list[11], 71), 0)
    pos_embed = draw_pos_embed(jax.random.fold_in(key_list[11], 71), 0)
    mod_shift = gaussian(key_list[9], (D,), 0.5, 2.0, (), jnp.float32)
    mod_scale = gaussian(key_list[10], (D,), 0.5, 2.0, (), jnp.float32)
    return dict(spatial_q=spatial_q, spatial_k=spatial_k, spatial_v=spatial_v, residual=residual, neighbour_list=neighbour_list, block_mask=block_mask, out_weight=out_weight, qkv_weight=qkv_weight, pos_embed=pos_embed, mod_shift=mod_shift, mod_scale=mod_scale)


EPS = 1e-06

def tiles_of(field):
    leading = field.shape[:-3]
    height, breadth, channels = field.shape[-3:]
    tile_grid = field.reshape(leading + (height // TILE, TILE, breadth // TILE, TILE, channels))
    lead_count = len(leading)
    arrangement = tuple(range(lead_count)) + (lead_count, lead_count + 2, lead_count + 1, lead_count + 3, lead_count + 4)
    tile_grid = jnp.transpose(tile_grid, arrangement)
    return tile_grid.reshape(leading + (height // TILE * (breadth // TILE), TILE * TILE, channels))

def untile(tiles, height, breadth):
    leading = tiles.shape[:-3]
    channels = tiles.shape[-1]
    tile_grid = tiles.reshape(leading + (height // TILE, breadth // TILE, TILE, TILE, channels))
    lead_count = len(leading)
    arrangement = tuple(range(lead_count)) + (lead_count, lead_count + 2, lead_count + 1, lead_count + 3, lead_count + 4)
    return jnp.transpose(tile_grid, arrangement).reshape(leading + (height, breadth, channels))

def window_attention(queries, keys, values):
    tile_count, token_count, channels = queries.shape
    head_size = channels // HEADS
    shaped_q = queries.astype(jnp.float32).reshape(tile_count, token_count, HEADS, head_size)
    shaped_k = keys.astype(jnp.float32).reshape(tile_count, -1, HEADS, head_size)
    shaped_v = values.astype(jnp.float32).reshape(tile_count, -1, HEADS, head_size)
    scores = jnp.einsum('tqhe,tkhe->thqk', shaped_q, shaped_k) * (1.0 / math.sqrt(head_size))
    peak = lax.optimization_barrier(jnp.max(scores, axis=-1, keepdims=True))
    powers = jnp.exp(scores - peak)
    weights = (powers / lax.optimization_barrier(jnp.sum(powers, axis=-1, keepdims=True))).astype(jnp.bfloat16)
    weights = lax.optimization_barrier(weights)
    mixed = jnp.einsum('thqk,tkhe->tqhe', weights.astype(jnp.float32), shaped_v)
    return mixed.astype(jnp.bfloat16).reshape(tile_count, token_count, channels)

def frame_attention(queries, keys, values, allowed):
    frame_count, spot_count, channels = queries.shape
    head_size = channels // HEADS
    shaped_q = queries.astype(jnp.float32).reshape(frame_count, spot_count, HEADS, head_size)
    shaped_k = keys.astype(jnp.float32).reshape(frame_count, spot_count, HEADS, head_size)
    shaped_v = values.astype(jnp.float32).reshape(frame_count, spot_count, HEADS, head_size)
    scores = jnp.einsum('fphe,gphe->phfg', shaped_q, shaped_k) * (1.0 / math.sqrt(head_size))
    scores = jnp.where(allowed, scores, -jnp.inf)
    peak = lax.optimization_barrier(jnp.max(scores, axis=-1, keepdims=True))
    powers = jnp.exp(scores - peak)
    weights = (powers / lax.optimization_barrier(jnp.sum(powers, axis=-1, keepdims=True))).astype(jnp.bfloat16)
    weights = lax.optimization_barrier(weights)
    mixed = jnp.einsum('phfg,gphe->fphe', weights.astype(jnp.float32), shaped_v)
    return mixed.astype(jnp.bfloat16).reshape(frame_count, spot_count, channels)

def normalize(field, mod_shift, mod_scale):
    average = lax.optimization_barrier(jnp.mean(field, axis=-1, keepdims=True))
    centred = field - average
    spread = lax.optimization_barrier(jnp.mean(centred * centred, axis=-1, keepdims=True))
    return centred * lax.rsqrt(spread + EPS) * (1.0 + mod_scale) + mod_shift

def by_clip(field):
    rolled = jnp.roll(field, TILE, axis=1)
    shaped = rolled.reshape(FRAMES, CLIPS, ROWS, COLS, D)
    return jnp.transpose(shaped, (1, 0, 2, 3, 4))

def reference(spatial_q, spatial_k, spatial_v, residual, neighbour_list, block_mask, out_weight, qkv_weight, pos_embed, mod_shift, mod_scale):
    allowed = jnp.repeat(jnp.repeat(block_mask, BLOCK, axis=0), BLOCK, axis=1) == 1
    spots = ROWS * COLS
    block_spots = TILE * COLS

    def clip_pass(clip_items):
        clip_q, clip_k, clip_v, clip_x, clip_list = clip_items

        def spatial_frame(items):
            frame_q, frame_k, frame_v, frame_x, frame_pos = items
            tiles_q = tiles_of(frame_q)
            tiles_k = jnp.take(tiles_of(frame_k), clip_list, axis=0).reshape(TILES, SLOTS * TILE * TILE, D)
            tiles_v = jnp.take(tiles_of(frame_v), clip_list, axis=0).reshape(TILES, SLOTS * TILE * TILE, D)
            heads = untile(window_attention(tiles_q, tiles_k, tiles_v), ROWS, COLS).reshape(ROWS * COLS, D)
            spatial_sum = jnp.dot(heads, out_weight, preferred_element_type=jnp.float32)
            mixed = (frame_x.reshape(ROWS * COLS, D).astype(jnp.float32) + spatial_sum).astype(jnp.bfloat16)
            mixed = lax.optimization_barrier(mixed)
            shifted = mixed.astype(jnp.float32) + frame_pos[None, :]
            return normalize(shifted, mod_shift, mod_scale).astype(jnp.bfloat16)
        normed_all = lax.map(spatial_frame, (clip_q, clip_k, clip_v, clip_x, pos_embed))
        grouped = jnp.transpose(normed_all.reshape(FRAMES, spots // block_spots, block_spots, D), (1, 0, 2, 3))

        def temporal_block(rows_block):
            projected = jnp.dot(rows_block.reshape(-1, D), qkv_weight, preferred_element_type=jnp.float32).astype(jnp.bfloat16)
            projected = lax.optimization_barrier(projected)
            projected = projected.reshape(FRAMES, block_spots, 3 * D)
            return frame_attention(projected[..., :D], projected[..., D:2 * D], projected[..., 2 * D:], allowed)
        mixed_blocks = lax.map(temporal_block, grouped)
        return jnp.transpose(mixed_blocks, (1, 0, 2, 3)).reshape(FRAMES, ROWS, COLS, D)
    lists = jnp.roll(neighbour_list, TILES_WIDE, axis=0).reshape(CLIPS, TILES, SLOTS)
    results = lax.map(clip_pass, (by_clip(spatial_q), by_clip(spatial_k), by_clip(spatial_v), by_clip(residual), lists))
    stacked = jnp.transpose(results, (1, 0, 2, 3, 4)).reshape(FRAMES, CLIPS * ROWS, COLS, D)
    return jnp.roll(stacked, -TILE, axis=1)
```

```python
import functools
import math

import jax
import jax.numpy as jnp
from jax import lax
from jax.experimental import pallas as pl
from jax.experimental.pallas import tpu as pltpu
from jax.sharding import PartitionSpec as P

HEADS = 16
TILE = 8
SLOTS = 6
ROWS = 32
BLOCK = 4
EPS = 1e-06
MESH = pl.DeviceIdType.MESH
F32 = jnp.float32
BF16 = jnp.bfloat16

GROUPS = ((0, 384, 0, 2), (384, 384, 2, 5), (768, 384, 5, 8))
BACK = ((0, 3, 0, 384), (3, 6, 384, 384), (6, 8, 768, 384))
SLAB = 384


def pair_masks(pair, head, dtype):
    lane = lax.broadcasted_iota(jnp.int32, (1, 256), 1) - 2 * (head - 64) * pair
    first = ((lane >= 0) & (lane < head)).astype(F32)
    second = ((lane >= head) & (lane < 2 * head)).astype(F32)
    return first.astype(dtype), second.astype(dtype)


def to_tiles(rows):
    wide = rows.astype(F32)
    return [
        wide[:, w * TILE : (w + 1) * TILE, :].reshape(TILE * TILE, wide.shape[-1])
        for w in range(rows.shape[1] // TILE)
    ]


def kernel(
    count,
    rows_axis,
    q_ref,
    k_ref,
    v_ref,
    res_ref,
    list_ref,
    mask_ref,
    wo_hbm,
    wq_hbm,
    pos_ref,
    shift_ref,
    scale_ref,
    out_ref,
    halo_k,
    halo_v,
    tiles_q,
    tiles_k,
    tiles_v,
    wo,
    wq,
    heads,
    mix,
    normed,
    xin,
    proj,
    tmix,
    back,
    bias,
    halo_send,
    halo_recv,
    own_sem,
    direct_send,
    pass_send,
    w_recv,
    go_send,
    go_recv,
    back_send,
    back_recv,
):
    frames_here, height, breadth, channels = q_ref.shape
    head = channels // HEADS
    spots = height * breadth
    piece = spots // count
    parts = piece // 16
    tiles_wide = breadth // TILE
    tile_rows = ROWS // TILE
    depth = wo_hbm.shape[0]
    chips = count // 2
    me = lax.axis_index("frame")
    row = lax.axis_index("row")
    core = me % 2
    chip = me // 2
    sibling = me + 1 - 2 * core
    up = (row + rows_axis - 1) % rows_axis
    down = (row + 1) % rows_axis
    tile_row = (row + 1) % tile_rows
    has_up = tile_row > 0
    has_down = tile_row < tile_rows - 1
    scale = math.log2(math.e) / math.sqrt(head)

    barrier = pltpu.get_barrier_semaphore()

    def greet(d, c):
        pl.semaphore_signal(
            barrier, inc=1, device_id={"frame": (me + d) % count}, device_id_type=MESH
        )
        return c

    lax.fori_loop(1, count, greet, 0)

    @pl.when(has_up)
    def _():
        pl.semaphore_signal(barrier, inc=1, device_id={"row": up}, device_id_type=MESH)

    @pl.when(has_down)
    def _():
        pl.semaphore_signal(barrier, inc=1, device_id={"row": down}, device_id_type=MESH)

    peers = count - 1 + (tile_row + tile_rows - 1) // tile_rows
    peers = peers + (2 * tile_rows - 2 - tile_row) // tile_rows
    pl.semaphore_wait(barrier, peers)

    def halo(slot, f, g, t):
        lanes = pl.ds(GROUPS[g][0], GROUPS[g][1])
        source = (k_ref, v_ref)[t]
        target = (halo_k, halo_v)[t]
        return pltpu.make_async_remote_copy(
            src_ref=source.at[f, :, :, lanes],
            dst_ref=target.at[slot, f, :, :, lanes],
            send_sem=halo_send.at[slot, f, g, t],
            recv_sem=halo_recv.at[slot, f, g, t],
            device_id={"row": down if slot == 0 else up},
            device_id_type=MESH,
        )

    halos = [
        (f, g, t) for f in range(frames_here) for g in range(len(GROUPS)) for t in range(2)
    ]

    def each_halo(step):
        for f, g, t in halos:

            @pl.when(has_up)
            def _():
                step(halo(1, f, g, t))

            @pl.when(has_down)
            def _():
                step(halo(0, f, g, t))

    each_halo(lambda copy: copy.start())

    weights = ((wo_hbm, wo), (wq_hbm, wq))

    def direct(i, d):
        other = ((chip + d) % chips) * 2 + core
        return pltpu.make_async_remote_copy(
            src_ref=weights[i][0],
            dst_ref=weights[i][1].at[me],
            send_sem=direct_send.at[i, d],
            recv_sem=w_recv.at[i, me],
            device_id={"frame": other},
            device_id_type=MESH,
        )

    def handed(i, d):
        shard = ((chip + d) % chips) * 2 + core
        return pltpu.make_async_remote_copy(
            src_ref=weights[i][1].at[shard],
            dst_ref=weights[i][1].at[shard],
            send_sem=pass_send.at[i, d],
            recv_sem=w_recv.at[i, shard],
            device_id={"frame": sibling},
            device_id_type=MESH,
        )

    def own_to_sibling(i):
        return pltpu.make_async_remote_copy(
            src_ref=weights[i][0],
            dst_ref=weights[i][1].at[me],
            send_sem=pass_send.at[i, 0],
            recv_sem=w_recv.at[i, me],
            device_id={"frame": sibling},
            device_id_type=MESH,
        )

    def arrival(i, shard):
        return pltpu.make_async_remote_copy(
            src_ref=weights[i][0],
            dst_ref=weights[i][1].at[shard],
            send_sem=pass_send.at[i, 0],
            recv_sem=w_recv.at[i, shard],
            device_id={"frame": sibling},
            device_id_type=MESH,
        )

    for i in range(2):
        pltpu.make_async_copy(weights[i][0], weights[i][1].at[me], own_sem.at[i]).start()
        for d in range(1, chips):
            direct(i, d).start()
        own_to_sibling(i).start()

    def hand_on(i):
        for d in range(1, chips):
            arrival(i, ((chip + d) % chips) * 2 + core).wait_recv()
            handed(i, d).start()

    def finish_weights(i):
        for d in range(chips):
            arrival(i, ((chip + d) % chips) * 2 + 1 - core).wait_recv()
        pltpu.make_async_copy(weights[i][0], weights[i][1].at[me], own_sem.at[i]).wait()

    def weight_slab(ref, lanes):
        if depth % 16 == 0:
            return ref[:, :, lanes].reshape(channels, SLAB)
        return jnp.concatenate([ref[s, :, lanes].astype(F32) for s in range(count)]).astype(BF16)

    def go(f, n):
        return pltpu.make_async_remote_copy(
            src_ref=normed.at[f, pl.ds(n * parts, parts)],
            dst_ref=xin.at[f, :, me],
            send_sem=go_send.at[f, n],
            recv_sem=go_recv.at[f, me],
            device_id={"frame": n},
            device_id_type=MESH,
        )

    def come(f, n):
        return pltpu.make_async_remote_copy(
            src_ref=normed.at[f, pl.ds(n * parts, parts)],
            dst_ref=xin.at[f, :, n],
            send_sem=go_send.at[f, n],
            recv_sem=go_recv.at[f, n],
            device_id={"frame": n},
            device_id_type=MESH,
        )

    def send_back(g, n):
        lanes = pl.ds(BACK[g][2], BACK[g][3])
        return pltpu.make_async_remote_copy(
            src_ref=tmix.at[:, :, n, :, lanes],
            dst_ref=back.at[:, pl.ds(me * parts, parts), :, lanes],
            send_sem=back_send.at[g, n],
            recv_sem=back_recv.at[g, me],
            device_id={"frame": n},
            device_id_type=MESH,
        )

    def come_back(g, n):
        lanes = pl.ds(BACK[g][2], BACK[g][3])
        return pltpu.make_async_remote_copy(
            src_ref=tmix.at[:, :, n, :, lanes],
            dst_ref=back.at[:, pl.ds(n * parts, parts), :, lanes],
            send_sem=back_send.at[g, n],
            recv_sem=back_recv.at[g, n],
            device_id={"frame": n},
            device_id_type=MESH,
        )

    def others(step):
        def body(d, c):
            step((me + d) % count)
            return c

        lax.fori_loop(1, count, body, 0)

    rows_t = frames_here * count * 16
    blocks = frames_here * count // BLOCK
    key_id = lax.broadcasted_iota(jnp.int32, (1, rows_t), 1)
    key_block = ((key_id // 16) % count) * 2 // BLOCK
    row_id = lax.broadcasted_iota(jnp.int32, (16 * BLOCK // 2, rows_t), 0)
    col_id = lax.broadcasted_iota(jnp.int32, (16 * BLOCK // 2, rows_t), 1)
    same = (row_id % 16) == (col_id % 16)
    for i in range(blocks):
        allowed = jnp.zeros((1, rows_t), jnp.int32)
        for j in range(blocks):
            allowed = jnp.where(key_block == j, mask_ref[i, j], allowed)
        plane = jnp.where(same & (allowed == 1), 0.0, -1e30).astype(F32)
        for f in range(frames_here):
            start = f * count * 16 + i * 16 * BLOCK // 2
            bias[start : start + 16 * BLOCK // 2, :] = plane

    def put_tiles(dst, first, rows, lanes):
        for w, tile in enumerate(to_tiles(rows)):
            dst[first + w, :, lanes] = tile.astype(BF16)

    def spatial_step(f, g):
        lanes = pl.ds(GROUPS[g][0], GROUPS[g][1])
        put_tiles(tiles_q, 0, q_ref[f, :, :, lanes], lanes)
        put_tiles(tiles_k, tiles_wide, k_ref[f, :, :, lanes], lanes)
        put_tiles(tiles_v, tiles_wide, v_ref[f, :, :, lanes], lanes)

        @pl.when(has_up)
        def _():
            halo(0, f, g, 0).wait_recv()
            put_tiles(tiles_k, 0, halo_k[0, f, :, :, lanes], lanes)
            halo(0, f, g, 1).wait_recv()
            put_tiles(tiles_v, 0, halo_v[0, f, :, :, lanes], lanes)

        @pl.when(has_down)
        def _():
            halo(1, f, g, 0).wait_recv()
            put_tiles(tiles_k, 2 * tiles_wide, halo_k[1, f, :, :, lanes], lanes)
            halo(1, f, g, 1).wait_recv()
            put_tiles(tiles_v, 2 * tiles_wide, halo_v[1, f, :, :, lanes], lanes)

        def pair_body(p, c):
            window = pl.ds(pl.multiple_of(p * 128, 128), 256)
            first, second = pair_masks(p, head, BF16)
            first32, second32 = pair_masks(p, head, F32)
            for w in range(tiles_wide):
                picks = [
                    jnp.clip(list_ref[w, s] - (tile_row - 1) * tiles_wide, 0, 3 * tiles_wide - 1)
                    for s in range(SLOTS)
                ]
                query = tiles_q[w, :, window]
                query = jnp.concatenate([query * first, query * second], axis=0)
                keys = jnp.concatenate([tiles_k[i, :, window] for i in picks], axis=0)
                values = jnp.concatenate([tiles_v[i, :, window] for i in picks], axis=0)
                s = lax.dot_general(
                    query, keys, (((1,), (1,)), ((), ())), preferred_element_type=F32
                )
                peak = jnp.max(s, axis=-1, keepdims=True)
                e = jnp.exp2((s - peak) * scale)
                e = e * (1.0 / jnp.sum(e, axis=-1, keepdims=True))
                o = jnp.dot(e.astype(BF16), values, preferred_element_type=F32)
                o = o[:64] * first32 + o[64:] * second32
                heads[w, :, window] += o.astype(BF16)
            return c

        lax.fori_loop(GROUPS[g][2], GROUPS[g][3], pair_body, 0)

    def project_out(f):
        x = heads[...].reshape(spots, channels)
        for n in range(channels // SLAB):
            lanes = pl.ds(n * SLAB, SLAB)
            y = jnp.dot(x, weight_slab(wo, lanes), preferred_element_type=F32)
            for w, tile in enumerate(to_tiles(res_ref[f, :, :, lanes])):
                mix[w, :, lanes] = tile + y[w * 64 : (w + 1) * 64]

        def norm_body(w, c):
            x = mix[w].astype(BF16).astype(F32) + pos_ref[f : f + 1, :]
            centred = x - jnp.mean(x, axis=-1, keepdims=True)
            spread = jnp.mean(centred * centred, axis=-1, keepdims=True)
            y = centred * lax.rsqrt(spread + EPS) * (1.0 + scale_ref[...]) + shift_ref[...]
            normed[f, pl.ds(w * 4, 4)] = y.astype(BF16).reshape(4, 16, channels)
            return c

        lax.fori_loop(0, tiles_wide, norm_body, 0)
        others(lambda n: go(f, n).start())
        xin[f, :, me] = normed[f, pl.ds(me * parts, parts)]

    for f in range(frames_here):
        heads[...] = jnp.zeros_like(heads)
        for g in range(len(GROUPS)):
            spatial_step(f, g)
            if f == 0 and g == 0:
                hand_on(0)
            if f == 0 and g == 2:
                finish_weights(0)
            if f == 1 and g == 0:
                hand_on(1)
        project_out(f)

    tmix[...] = jnp.zeros_like(tmix)
    finish_weights(1)

    def project_in(f):
        others(lambda n: come(f, n).wait_recv())
        x = xin[f].reshape(piece * count, channels)

        def slab_body(n, c):
            lanes = pl.ds(pl.multiple_of(n * SLAB, 128), SLAB)
            y = jnp.dot(x, weight_slab(wq, lanes), preferred_element_type=F32)
            proj[f, :, :, lanes] = y.astype(BF16).reshape(parts, count * 16, SLAB)
            return c

        lax.fori_loop(0, 3 * channels // SLAB, slab_body, 0)

    for f in range(frames_here):
        project_in(f)

    def temporal_pair(p, c):
        start = pl.multiple_of(p * 128, 128)
        window = pl.ds(start, 256)
        masks = pair_masks(p, head, BF16)
        masks32 = pair_masks(p, head, F32)
        for b in range(parts):
            query = proj[:, b, :, window].reshape(rows_t, 256)
            keys = proj[:, b, :, pl.ds(start + channels, 256)].reshape(rows_t, 256)
            values = proj[:, b, :, pl.ds(start + 2 * channels, 256)].reshape(rows_t, 256)
            total = 0.0
            for h in range(2):
                s = lax.dot_general(
                    query * masks[h],
                    keys,
                    (((1,), (1,)), ((), ())),
                    preferred_element_type=F32,
                )
                s = s + bias[...]
                peak = jnp.max(s, axis=-1, keepdims=True)
                e = jnp.exp2((s - peak) * scale)
                e = e * (1.0 / jnp.sum(e, axis=-1, keepdims=True))
                o = jnp.dot(e.astype(BF16), values, preferred_element_type=F32)
                total = total + o * masks32[h]
            tmix[:, b, :, :, window] += total.astype(BF16).reshape(frames_here, count, 16, 256)
        return c

    for g, (p0, p1, lane0, width) in enumerate(BACK):
        lax.fori_loop(p0, p1, temporal_pair, 0)
        others(lambda n: send_back(g, n).start())
        lanes = pl.ds(lane0, width)
        back[:, pl.ds(me * parts, parts), :, lanes] = tmix[:, :, me, :, lanes]

    for g, (p0, p1, lane0, width) in enumerate(BACK):
        others(lambda n: come_back(g, n).wait_recv())
        lanes = pl.ds(lane0, width)
        for f in range(frames_here):
            for i in range(height // 2):
                got = [
                    back[f, w * (height // 2) + i, :, lanes].astype(F32)
                    for w in range(tiles_wide)
                ]
                for half in range(2):
                    out_ref[f, 2 * i + half, :, lanes] = jnp.concatenate(
                        [x[half * 8 : half * 8 + 8] for x in got], axis=0
                    ).astype(BF16)

    each_halo(lambda copy: copy.wait_send())
    for i in range(2):
        for d in range(1, chips):
            direct(i, d).wait_send()
            handed(i, d).wait_send()
        own_to_sibling(i).wait_send()
    for f in range(frames_here):
        others(lambda n: go(f, n).wait_send())
    for g in range(len(BACK)):
        others(lambda n: send_back(g, n).wait_send())


def local(
    count,
    rows_axis,
    spatial_q,
    spatial_k,
    spatial_v,
    residual,
    neighbour_list,
    block_mask,
    out_weight,
    qkv_weight,
    pos_embed,
    mod_shift,
    mod_scale,
):
    frames_here, height, breadth, channels = spatial_q.shape
    tiles_wide = breadth // TILE
    spots = height * breadth
    parts = spots // count // 16
    chips = count // 2
    depth = out_weight.shape[0]
    groups = len(GROUPS)
    rows_t = frames_here * count * 16
    vmem = pl.BlockSpec(memory_space=pltpu.VMEM)
    smem = pl.BlockSpec(memory_space=pltpu.SMEM)
    hbm = pl.BlockSpec(memory_space=pl.ANY)
    dma = pltpu.SemaphoreType.DMA
    return pl.pallas_call(
        functools.partial(kernel, count, rows_axis),
        out_shape=jax.ShapeDtypeStruct(spatial_q.shape, BF16),
        in_specs=[vmem, vmem, vmem, vmem, smem, smem, hbm, hbm, vmem, vmem, vmem],
        out_specs=vmem,
        scratch_shapes=[
            pltpu.VMEM((2, frames_here, height, breadth, channels), BF16),
            pltpu.VMEM((2, frames_here, height, breadth, channels), BF16),
            pltpu.VMEM((tiles_wide, 64, channels), BF16),
            pltpu.VMEM((3 * tiles_wide, 64, channels), BF16),
            pltpu.VMEM((3 * tiles_wide, 64, channels), BF16),
            pltpu.VMEM((count, depth, channels), BF16),
            pltpu.VMEM((count, depth, 3 * channels), BF16),
            pltpu.VMEM((tiles_wide, 64, channels), BF16),
            pltpu.VMEM((tiles_wide, 64, channels), F32),
            pltpu.VMEM((frames_here, spots // 16, 16, channels), BF16),
            pltpu.VMEM((frames_here, parts, count, 16, channels), BF16),
            pltpu.VMEM((frames_here, parts, count * 16, 3 * channels), BF16),
            pltpu.VMEM((frames_here, parts, count, 16, channels), BF16),
            pltpu.VMEM((frames_here, spots // 16, 16, channels), BF16),
            pltpu.VMEM((rows_t, rows_t), F32),
            dma((2, frames_here, groups, 2)),
            dma((2, frames_here, groups, 2)),
            dma((2,)),
            dma((2, chips)),
            dma((2, chips)),
            dma((2, count)),
            dma((frames_here, count)),
            dma((frames_here, count)),
            dma((len(BACK), count)),
            dma((len(BACK), count)),
        ],
        compiler_params=pltpu.CompilerParams(
            collective_id=0, has_side_effects=True, vmem_limit_bytes=60 * 2**20
        ),
    )(
        spatial_q,
        spatial_k,
        spatial_v,
        residual,
        neighbour_list,
        block_mask,
        out_weight,
        qkv_weight,
        pos_embed,
        mod_shift.reshape(1, channels),
        mod_scale.reshape(1, channels),
    )


def solution(mesh):
    return jax.shard_map(
        functools.partial(local, mesh.shape["frame"], mesh.shape["row"]),
        mesh=mesh,
        in_specs=(
            P("frame", "row", None, None),
            P("frame", "row", None, None),
            P("frame", "row", None, None),
            P("frame", "row", None, None),
            P("row", None),
            P(),
            P("frame", None),
            P("frame", None),
            P("frame", None),
            P(),
            P(),
        ),
        out_specs=P("frame", "row", None, None),
        check_vma=False,
    )
```

```python
import functools
import math

import jax
import jax.numpy as jnp
from jax import lax
from jax.experimental import pallas as pl
from jax.experimental.pallas import tpu as pltpu
from jax.sharding import PartitionSpec as P

HEADS = 16
TILE = 8
SLOTS = 6
ROWS = 32
BLOCK = 4
EPS = 1e-06
MESH = pl.DeviceIdType.MESH
F32 = jnp.float32
BF16 = jnp.bfloat16

GROUPS = ((0, 384, 0, 2), (384, 384, 2, 5), (768, 384, 5, 8))
BACK = ((0, 3, 0, 384), (3, 6, 384, 384), (6, 8, 768, 384))
SLAB = 384


def pair_masks(pair, head, dtype):
    lane = lax.broadcasted_iota(jnp.int32, (1, 256), 1) - 2 * (head - 64) * pair
    first = ((lane >= 0) & (lane < head)).astype(F32)
    second = ((lane >= head) & (lane < 2 * head)).astype(F32)
    return first.astype(dtype), second.astype(dtype)


def to_tiles(rows):
    wide = rows.astype(F32)
    return [
        wide[:, w * TILE : (w + 1) * TILE, :].reshape(TILE * TILE, wide.shape[-1])
        for w in range(rows.shape[1] // TILE)
    ]


def kernel(
    count,
    rows_axis,
    q_hbm,
    k_hbm,
    v_hbm,
    res_hbm,
    list_ref,
    mask_ref,
    wo_hbm,
    wq_hbm,
    pos_ref,
    shift_ref,
    scale_ref,
    out_ref,
    q_ref,
    k_ref,
    v_ref,
    res_ref,
    halo_k,
    halo_v,
    tiles_q,
    tiles_k,
    tiles_v,
    wo,
    wq,
    heads,
    mix,
    normed,
    xin,
    proj,
    tmix,
    back,
    bias,
    halo_send,
    halo_recv,
    own_sem,
    in_sem,
    direct_send,
    pass_send,
    w_recv,
    go_send,
    go_recv,
    back_send,
    back_recv,
):
    frames_here, height, breadth, channels = q_hbm.shape
    head = channels // HEADS
    spots = height * breadth
    piece = spots // count
    parts = piece // 16
    tiles_wide = breadth // TILE
    tile_rows = ROWS // TILE
    depth = wo_hbm.shape[0]
    chips = count // 2
    me = lax.axis_index("frame")
    row = lax.axis_index("row")
    core = me % 2
    chip = me // 2
    sibling = me + 1 - 2 * core
    up = (row + rows_axis - 1) % rows_axis
    down = (row + 1) % rows_axis
    tile_row = (row + 1) % tile_rows
    has_up = tile_row > 0
    has_down = tile_row < tile_rows - 1
    scale = math.log2(math.e) / math.sqrt(head)

    barrier = pltpu.get_barrier_semaphore()

    def greet(d, c):
        pl.semaphore_signal(
            barrier, inc=1, device_id={"frame": (me + d) % count}, device_id_type=MESH
        )
        return c

    lax.fori_loop(1, count, greet, 0)

    @pl.when(has_up)
    def _():
        pl.semaphore_signal(barrier, inc=1, device_id={"row": up}, device_id_type=MESH)

    @pl.when(has_down)
    def _():
        pl.semaphore_signal(barrier, inc=1, device_id={"row": down}, device_id_type=MESH)

    peers = count - 1 + (tile_row + tile_rows - 1) // tile_rows
    peers = peers + (2 * tile_rows - 2 - tile_row) // tile_rows
    pl.semaphore_wait(barrier, peers)

    def halo(slot, f, g, t):
        lanes = pl.ds(GROUPS[g][0], GROUPS[g][1])
        source = (k_hbm, v_hbm)[t]
        target = (halo_k, halo_v)[t]
        return pltpu.make_async_remote_copy(
            src_ref=source.at[f, :, :, lanes],
            dst_ref=target.at[slot, f, :, :, lanes],
            send_sem=halo_send.at[slot, f, g, t],
            recv_sem=halo_recv.at[slot, f, g, t],
            device_id={"row": down if slot == 0 else up},
            device_id_type=MESH,
        )

    halos = [
        (f, g, t) for f in range(frames_here) for g in range(len(GROUPS)) for t in range(2)
    ]

    def each_halo(step, chosen=halos):
        for f, g, t in chosen:

            @pl.when(has_up)
            def _():
                step(halo(1, f, g, t))

            @pl.when(has_down)
            def _():
                step(halo(0, f, g, t))

    def start_halos(f, g):
        each_halo(lambda copy: copy.start(), [(f, g, 0), (f, g, 1)])

    inputs = [
        pltpu.make_async_copy(source, target, in_sem.at[i])
        for i, (source, target) in enumerate(
            ((q_hbm, q_ref), (k_hbm, k_ref), (v_hbm, v_ref), (res_hbm, res_ref))
        )
    ]
    start_halos(0, 0)
    start_halos(0, 1)
    for copy in inputs:
        copy.start()

    weights = ((wo_hbm, wo), (wq_hbm, wq))

    def direct(i, d):
        other = ((chip + d) % chips) * 2 + core
        return pltpu.make_async_remote_copy(
            src_ref=weights[i][0],
            dst_ref=weights[i][1].at[me],
            send_sem=direct_send.at[i, d],
            recv_sem=w_recv.at[i, me],
            device_id={"frame": other},
            device_id_type=MESH,
        )

    def handed(i, d):
        shard = ((chip + d) % chips) * 2 + core
        return pltpu.make_async_remote_copy(
            src_ref=weights[i][1].at[shard],
            dst_ref=weights[i][1].at[shard],
            send_sem=pass_send.at[i, d],
            recv_sem=w_recv.at[i, shard],
            device_id={"frame": sibling},
            device_id_type=MESH,
        )

    def own_to_sibling(i):
        return pltpu.make_async_remote_copy(
            src_ref=weights[i][0],
            dst_ref=weights[i][1].at[me],
            send_sem=pass_send.at[i, 0],
            recv_sem=w_recv.at[i, me],
            device_id={"frame": sibling},
            device_id_type=MESH,
        )

    def arrival(i, shard):
        return pltpu.make_async_remote_copy(
            src_ref=weights[i][0],
            dst_ref=weights[i][1].at[shard],
            send_sem=pass_send.at[i, 0],
            recv_sem=w_recv.at[i, shard],
            device_id={"frame": sibling},
            device_id_type=MESH,
        )

    for i in range(2):
        pltpu.make_async_copy(weights[i][0], weights[i][1].at[me], own_sem.at[i]).start()
        for d in range(1, chips):
            direct(i, d).start()
        own_to_sibling(i).start()

    start_halos(0, 2)

    def hand_on(i):
        for d in range(1, chips):
            arrival(i, ((chip + d) % chips) * 2 + core).wait_recv()
            handed(i, d).start()

    def finish_weights(i):
        for d in range(chips):
            arrival(i, ((chip + d) % chips) * 2 + 1 - core).wait_recv()
        pltpu.make_async_copy(weights[i][0], weights[i][1].at[me], own_sem.at[i]).wait()

    def weight_slab(ref, lanes):
        if depth % 16 == 0:
            return ref[:, :, lanes].reshape(channels, SLAB)
        return jnp.concatenate([ref[s, :, lanes].astype(F32) for s in range(count)]).astype(BF16)

    def go(f, n):
        return pltpu.make_async_remote_copy(
            src_ref=normed.at[f, pl.ds(n * parts, parts)],
            dst_ref=xin.at[f, :, me],
            send_sem=go_send.at[f, n],
            recv_sem=go_recv.at[f, me],
            device_id={"frame": n},
            device_id_type=MESH,
        )

    def come(f, n):
        return pltpu.make_async_remote_copy(
            src_ref=normed.at[f, pl.ds(n * parts, parts)],
            dst_ref=xin.at[f, :, n],
            send_sem=go_send.at[f, n],
            recv_sem=go_recv.at[f, n],
            device_id={"frame": n},
            device_id_type=MESH,
        )

    def send_back(g, n):
        lanes = pl.ds(BACK[g][2], BACK[g][3])
        return pltpu.make_async_remote_copy(
            src_ref=tmix.at[:, :, n, :, lanes],
            dst_ref=back.at[:, pl.ds(me * parts, parts), :, lanes],
            send_sem=back_send.at[g, n],
            recv_sem=back_recv.at[g, me],
            device_id={"frame": n},
            device_id_type=MESH,
        )

    def come_back(g, n):
        lanes = pl.ds(BACK[g][2], BACK[g][3])
        return pltpu.make_async_remote_copy(
            src_ref=tmix.at[:, :, n, :, lanes],
            dst_ref=back.at[:, pl.ds(n * parts, parts), :, lanes],
            send_sem=back_send.at[g, n],
            recv_sem=back_recv.at[g, n],
            device_id={"frame": n},
            device_id_type=MESH,
        )

    def others(step):
        def body(d, c):
            step((me + d) % count)
            return c

        lax.fori_loop(1, count, body, 0)

    rows_t = frames_here * count * 8
    blocks = frames_here * count // BLOCK
    band = 8 * BLOCK // frames_here
    key_id = lax.broadcasted_iota(jnp.int32, (1, rows_t), 1)
    key_block = ((key_id // 8) % count) * frames_here // BLOCK
    row_id = lax.broadcasted_iota(jnp.int32, (band, rows_t), 0)
    col_id = lax.broadcasted_iota(jnp.int32, (band, rows_t), 1)
    same = (row_id % 8) == (col_id % 8)
    for i in range(blocks):
        allowed = jnp.zeros((1, rows_t), jnp.int32)
        for j in range(blocks):
            allowed = jnp.where(key_block == j, mask_ref[i, j], allowed)
        plane = jnp.where(same & (allowed == 1), 0.0, -1e30).astype(F32)
        for f in range(frames_here):
            start = f * count * 8 + i * band
            bias[start : start + band, :] = plane

    def put_tiles(dst, first, rows, lanes):
        for w, tile in enumerate(to_tiles(rows)):
            dst[first + w, :, lanes] = tile.astype(BF16)

    def spatial_step(f, g):
        lanes = pl.ds(GROUPS[g][0], GROUPS[g][1])
        put_tiles(tiles_q, 0, q_ref[f, :, :, lanes], lanes)
        put_tiles(tiles_k, tiles_wide, k_ref[f, :, :, lanes], lanes)
        put_tiles(tiles_v, tiles_wide, v_ref[f, :, :, lanes], lanes)

        @pl.when(has_up)
        def _():
            halo(0, f, g, 0).wait_recv()
            put_tiles(tiles_k, 0, halo_k[0, f, :, :, lanes], lanes)
            halo(0, f, g, 1).wait_recv()
            put_tiles(tiles_v, 0, halo_v[0, f, :, :, lanes], lanes)

        @pl.when(has_down)
        def _():
            halo(1, f, g, 0).wait_recv()
            put_tiles(tiles_k, 2 * tiles_wide, halo_k[1, f, :, :, lanes], lanes)
            halo(1, f, g, 1).wait_recv()
            put_tiles(tiles_v, 2 * tiles_wide, halo_v[1, f, :, :, lanes], lanes)

        def pair_body(p, c):
            window = pl.ds(pl.multiple_of(p * 128, 128), 256)
            first, second = pair_masks(p, head, BF16)
            first32, second32 = pair_masks(p, head, F32)
            for w in range(tiles_wide):
                picks = [
                    jnp.clip(list_ref[w, s] - (tile_row - 1) * tiles_wide, 0, 3 * tiles_wide - 1)
                    for s in range(SLOTS)
                ]
                query = tiles_q[w, :, window]
                query = jnp.concatenate([query * first, query * second], axis=0)
                keys = jnp.concatenate([tiles_k[i, :, window] for i in picks], axis=0)
                values = jnp.concatenate([tiles_v[i, :, window] for i in picks], axis=0)
                s = lax.dot_general(
                    query, keys, (((1,), (1,)), ((), ())), preferred_element_type=F32
                )
                peak = jnp.max(s, axis=-1, keepdims=True)
                e = jnp.exp2((s - peak) * scale)
                e = e * (1.0 / jnp.sum(e, axis=-1, keepdims=True))
                o = jnp.dot(e.astype(BF16), values, preferred_element_type=F32)
                o = o[:64] * first32 + o[64:] * second32
                heads[w, :, window] += o.astype(BF16)
            return c

        lax.fori_loop(GROUPS[g][2], GROUPS[g][3], pair_body, 0)

    def project_out(f):
        x = heads[...].reshape(spots, channels)
        for n in range(channels // SLAB):
            lanes = pl.ds(n * SLAB, SLAB)
            y = jnp.dot(x, weight_slab(wo, lanes), preferred_element_type=F32)
            for w, tile in enumerate(to_tiles(res_ref[f, :, :, lanes])):
                mix[w, :, lanes] = tile + y[w * 64 : (w + 1) * 64]

        gain = 1.0 + scale_ref[...].reshape(1, channels)
        offset = shift_ref[...].reshape(1, channels)

        def norm_body(w, c):
            x = mix[w].astype(BF16).astype(F32) + pos_ref[f : f + 1, :]
            centred = x - jnp.mean(x, axis=-1, keepdims=True)
            spread = jnp.mean(centred * centred, axis=-1, keepdims=True)
            y = centred * lax.rsqrt(spread + EPS) * gain + offset
            normed[f, pl.ds(w * 4, 4)] = y.astype(BF16).reshape(4, 16, channels)
            return c

        lax.fori_loop(0, tiles_wide, norm_body, 0)
        others(lambda n: go(f, n).start())
        xin[f, :, me] = normed[f, pl.ds(me * parts, parts)]

    for copy in inputs:
        copy.wait()
    for f in range(frames_here):
        heads[...] = jnp.zeros_like(heads)
        for g in range(len(GROUPS)):
            spatial_step(f, g)
            if f + 1 < frames_here:
                start_halos(f + 1, g)
            if f == 0 and g == 0:
                hand_on(0)
            if f == 0 and g == 2:
                finish_weights(0)
            if f == 1 and g == 0:
                hand_on(1)
        project_out(f)

    tmix[...] = jnp.zeros_like(tmix)
    finish_weights(1)

    def project_in(f):
        others(lambda n: come(f, n).wait_recv())
        x = xin[f].reshape(piece * count, channels)

        def slab_body(n, c):
            lanes = pl.ds(pl.multiple_of(n * SLAB, 128), SLAB)
            y = jnp.dot(x, weight_slab(wq, lanes), preferred_element_type=F32)
            y = y.reshape(parts, count, 2, 8, SLAB)
            for half in range(2):
                z = y[:, :, half].reshape(parts, count * 8, SLAB)
                proj[f, :, half, :, lanes] = z.astype(BF16)
            return c

        lax.fori_loop(0, 3 * channels // SLAB, slab_body, 0)

    for f in range(frames_here):
        project_in(f)

    def temporal_pair(p, c):
        start = pl.multiple_of(p * 128, 128)
        window = pl.ds(start, 256)
        masks = pair_masks(p, head, BF16)
        masks32 = pair_masks(p, head, F32)
        for b in range(parts):
            found = []
            for half in range(2):
                query = proj[:, b, half, :, window].reshape(rows_t, 256)
                keys = proj[:, b, half, :, pl.ds(start + channels, 256)].reshape(rows_t, 256)
                values = proj[:, b, half, :, pl.ds(start + 2 * channels, 256)]
                values = values.reshape(rows_t, 256)
                query = jnp.concatenate([query * masks[0], query * masks[1]], axis=0)
                s = lax.dot_general(
                    query, keys, (((1,), (1,)), ((), ())), preferred_element_type=F32
                )
                s = s.reshape(2, rows_t, rows_t) + bias[...]
                peak = jnp.max(s, axis=-1, keepdims=True)
                e = jnp.exp2((s - peak) * scale)
                e = e * (1.0 / jnp.sum(e, axis=-1, keepdims=True))
                e = e.astype(BF16).reshape(2 * rows_t, rows_t)
                o = jnp.dot(e, values, preferred_element_type=F32)
                o = o[:rows_t] * masks32[0] + o[rows_t:] * masks32[1]
                found.append(o.reshape(frames_here, count, 8, 256))
            both = jnp.stack(found, axis=2).reshape(frames_here, count, 16, 256)
            tmix[:, b, :, :, window] += both.astype(BF16)
        return c

    for g, (p0, p1, lane0, width) in enumerate(BACK):
        lax.fori_loop(p0, p1, temporal_pair, 0)
        others(lambda n: send_back(g, n).start())
        lanes = pl.ds(lane0, width)
        back[:, pl.ds(me * parts, parts), :, lanes] = tmix[:, :, me, :, lanes]

    for g, (p0, p1, lane0, width) in enumerate(BACK):
        others(lambda n: come_back(g, n).wait_recv())
        lanes = pl.ds(lane0, width)
        for f in range(frames_here):
            for i in range(height // 2):
                got = [
                    back[f, w * (height // 2) + i, :, lanes].astype(F32)
                    for w in range(tiles_wide)
                ]
                for half in range(2):
                    out_ref[f, 2 * i + half, :, lanes] = jnp.concatenate(
                        [x[half * 8 : half * 8 + 8] for x in got], axis=0
                    ).astype(BF16)

    each_halo(lambda copy: copy.wait_send())
    for i in range(2):
        for d in range(1, chips):
            direct(i, d).wait_send()
            handed(i, d).wait_send()
        own_to_sibling(i).wait_send()
    for f in range(frames_here):
        others(lambda n: go(f, n).wait_send())
    for g in range(len(BACK)):
        others(lambda n: send_back(g, n).wait_send())


def local(
    count,
    rows_axis,
    spatial_q,
    spatial_k,
    spatial_v,
    residual,
    neighbour_list,
    block_mask,
    out_weight,
    qkv_weight,
    pos_embed,
    mod_shift,
    mod_scale,
):
    frames_here, height, breadth, channels = spatial_q.shape
    tiles_wide = breadth // TILE
    spots = height * breadth
    parts = spots // count // 16
    chips = count // 2
    depth = out_weight.shape[0]
    groups = len(GROUPS)
    rows_t = frames_here * count * 8
    vmem = pl.BlockSpec(memory_space=pltpu.VMEM)
    smem = pl.BlockSpec(memory_space=pltpu.SMEM)
    hbm = pl.BlockSpec(memory_space=pl.ANY)
    dma = pltpu.SemaphoreType.DMA
    return pl.pallas_call(
        functools.partial(kernel, count, rows_axis),
        out_shape=jax.ShapeDtypeStruct(spatial_q.shape, BF16),
        in_specs=[hbm, hbm, hbm, hbm, smem, smem, hbm, hbm, vmem, vmem, vmem],
        out_specs=vmem,
        scratch_shapes=[
            pltpu.VMEM((frames_here, height, breadth, channels), BF16),
            pltpu.VMEM((frames_here, height, breadth, channels), BF16),
            pltpu.VMEM((frames_here, height, breadth, channels), BF16),
            pltpu.VMEM((frames_here, height, breadth, channels), BF16),
            pltpu.VMEM((2, frames_here, height, breadth, channels), BF16),
            pltpu.VMEM((2, frames_here, height, breadth, channels), BF16),
            pltpu.VMEM((tiles_wide, 64, channels), BF16),
            pltpu.VMEM((3 * tiles_wide, 64, channels), BF16),
            pltpu.VMEM((3 * tiles_wide, 64, channels), BF16),
            pltpu.VMEM((count, depth, channels), BF16),
            pltpu.VMEM((count, depth, 3 * channels), BF16),
            pltpu.VMEM((tiles_wide, 64, channels), BF16),
            pltpu.VMEM((tiles_wide, 64, channels), F32),
            pltpu.VMEM((frames_here, spots // 16, 16, channels), BF16),
            pltpu.VMEM((frames_here, parts, count, 16, channels), BF16),
            pltpu.VMEM((frames_here, parts, 2, count * 8, 3 * channels), BF16),
            pltpu.VMEM((frames_here, parts, count, 16, channels), BF16),
            pltpu.VMEM((frames_here, spots // 16, 16, channels), BF16),
            pltpu.VMEM((rows_t, rows_t), F32),
            dma((2, frames_here, groups, 2)),
            dma((2, frames_here, groups, 2)),
            dma((2,)),
            dma((4,)),
            dma((2, chips)),
            dma((2, chips)),
            dma((2, count)),
            dma((frames_here, count)),
            dma((frames_here, count)),
            dma((len(BACK), count)),
            dma((len(BACK), count)),
        ],
        compiler_params=pltpu.CompilerParams(
            collective_id=0, has_side_effects=True, vmem_limit_bytes=60 * 2**20
        ),
    )(
        spatial_q,
        spatial_k,
        spatial_v,
        residual,
        neighbour_list,
        block_mask,
        out_weight,
        qkv_weight,
        pos_embed,
        mod_shift,
        mod_scale,
    )


def solution(mesh):
    return jax.shard_map(
        functools.partial(local, mesh.shape["frame"], mesh.shape["row"]),
        mesh=mesh,
        in_specs=(
            P("frame", "row", None, None),
            P("frame", "row", None, None),
            P("frame", "row", None, None),
            P("frame", "row", None, None),
            P("row", None),
            P(),
            P("frame", None),
            P("frame", None),
            P("frame", None),
            P(),
            P(),
        ),
        out_specs=P("frame", "row", None, None),
        check_vma=False,
    )
```

```python
import functools
import math

import jax
import jax.numpy as jnp
from jax import lax
from jax.experimental import pallas as pl
from jax.experimental.pallas import tpu as pltpu
from jax.sharding import PartitionSpec as P

HEADS = 16
TILE = 8
SLOTS = 6
ROWS = 32
BLOCK = 4
EPS = 1e-06
MESH = pl.DeviceIdType.MESH
F32 = jnp.float32
BF16 = jnp.bfloat16

GROUPS = ((0, 512, 0, 3), (512, 384, 3, 6), (896, 256, 6, 8))
BACK = ((0, 3, 0, 384), (3, 6, 384, 384), (6, 8, 768, 384))
SLAB = 384


def pair_masks(pair, head, dtype):
    lane = lax.broadcasted_iota(jnp.int32, (1, 256), 1) - 2 * (head - 64) * pair
    first = ((lane >= 0) & (lane < head)).astype(F32)
    second = ((lane >= head) & (lane < 2 * head)).astype(F32)
    return first.astype(dtype), second.astype(dtype)


def to_tiles(rows):
    wide = rows.astype(F32)
    return [
        wide[:, w * TILE : (w + 1) * TILE, :].reshape(TILE * TILE, wide.shape[-1])
        for w in range(rows.shape[1] // TILE)
    ]


def kernel(
    count,
    rows_axis,
    q_hbm,
    k_hbm,
    v_hbm,
    res_hbm,
    list_ref,
    mask_ref,
    wo_hbm,
    wq_hbm,
    pos_ref,
    shift_ref,
    scale_ref,
    out_ref,
    q_ref,
    k_ref,
    v_ref,
    res_ref,
    halo_k,
    halo_v,
    tiles_q,
    tiles_k,
    tiles_v,
    wo,
    wq,
    heads,
    mix,
    normed,
    xin,
    proj,
    tmix,
    back,
    bias,
    halo_send,
    halo_recv,
    own_sem,
    in_sem,
    direct_send,
    pass_send,
    w_recv,
    go_send,
    go_recv,
    back_send,
    back_recv,
):
    frames_here, height, breadth, channels = q_hbm.shape
    head = channels // HEADS
    spots = height * breadth
    piece = spots // count
    parts = piece // 16
    tiles_wide = breadth // TILE
    tile_rows = ROWS // TILE
    depth = wo_hbm.shape[0]
    chips = count // 2
    me = lax.axis_index("frame")
    row = lax.axis_index("row")
    core = me % 2
    chip = me // 2
    sibling = me + 1 - 2 * core
    up = (row + rows_axis - 1) % rows_axis
    down = (row + 1) % rows_axis
    tile_row = (row + 1) % tile_rows
    has_up = tile_row > 0
    has_down = tile_row < tile_rows - 1
    scale = math.log2(math.e) / math.sqrt(head)

    barrier = pltpu.get_barrier_semaphore()

    def greet(d, c):
        pl.semaphore_signal(
            barrier, inc=1, device_id={"frame": (me + d) % count}, device_id_type=MESH
        )
        return c

    lax.fori_loop(1, count, greet, 0)

    @pl.when(has_up)
    def _():
        pl.semaphore_signal(barrier, inc=1, device_id={"row": up}, device_id_type=MESH)

    @pl.when(has_down)
    def _():
        pl.semaphore_signal(barrier, inc=1, device_id={"row": down}, device_id_type=MESH)

    peers = count - 1 + (tile_row + tile_rows - 1) // tile_rows
    peers = peers + (2 * tile_rows - 2 - tile_row) // tile_rows
    pl.semaphore_wait(barrier, peers)

    def halo(slot, f, g, t):
        lanes = pl.ds(GROUPS[g][0], GROUPS[g][1])
        source = (k_hbm, v_hbm)[t]
        target = (halo_k, halo_v)[t]
        return pltpu.make_async_remote_copy(
            src_ref=source.at[f, :, :, lanes],
            dst_ref=target.at[slot, f, :, :, lanes],
            send_sem=halo_send.at[slot, f, g, t],
            recv_sem=halo_recv.at[slot, f, g, t],
            device_id={"row": down if slot == 0 else up},
            device_id_type=MESH,
        )

    halos = [
        (f, g, t) for f in range(frames_here) for g in range(len(GROUPS)) for t in range(2)
    ]

    def each_halo(step, chosen=halos):
        for f, g, t in chosen:

            @pl.when(has_up)
            def _():
                step(halo(1, f, g, t))

            @pl.when(has_down)
            def _():
                step(halo(0, f, g, t))

    def start_halos(f, g):
        each_halo(lambda copy: copy.start(), [(f, g, 0), (f, g, 1)])

    inputs = [
        pltpu.make_async_copy(source, target, in_sem.at[i])
        for i, (source, target) in enumerate(
            ((q_hbm, q_ref), (k_hbm, k_ref), (v_hbm, v_ref), (res_hbm, res_ref))
        )
    ]
    for g in range(len(GROUPS)):
        start_halos(0, g)
    for copy in inputs:
        copy.start()

    weights = ((wo_hbm, wo), (wq_hbm, wq))

    def direct(i, d):
        other = ((chip + d) % chips) * 2 + core
        return pltpu.make_async_remote_copy(
            src_ref=weights[i][0],
            dst_ref=weights[i][1].at[me],
            send_sem=direct_send.at[i, d],
            recv_sem=w_recv.at[i, me],
            device_id={"frame": other},
            device_id_type=MESH,
        )

    def handed(i, d):
        shard = ((chip + d) % chips) * 2 + core
        return pltpu.make_async_remote_copy(
            src_ref=weights[i][1].at[shard],
            dst_ref=weights[i][1].at[shard],
            send_sem=pass_send.at[i, d],
            recv_sem=w_recv.at[i, shard],
            device_id={"frame": sibling},
            device_id_type=MESH,
        )

    def own_to_sibling(i):
        return pltpu.make_async_remote_copy(
            src_ref=weights[i][0],
            dst_ref=weights[i][1].at[me],
            send_sem=pass_send.at[i, 0],
            recv_sem=w_recv.at[i, me],
            device_id={"frame": sibling},
            device_id_type=MESH,
        )

    def arrival(i, shard):
        return pltpu.make_async_remote_copy(
            src_ref=weights[i][0],
            dst_ref=weights[i][1].at[shard],
            send_sem=pass_send.at[i, 0],
            recv_sem=w_recv.at[i, shard],
            device_id={"frame": sibling},
            device_id_type=MESH,
        )

    for i in range(2):
        pltpu.make_async_copy(weights[i][0], weights[i][1].at[me], own_sem.at[i]).start()
        for d in range(1, chips):
            direct(i, d).start()
        own_to_sibling(i).start()
        if i == 0:
            for f in range(1, frames_here):
                for g in range(len(GROUPS)):
                    start_halos(f, g)

    def hand_on(i):
        for d in range(1, chips):
            arrival(i, ((chip + d) % chips) * 2 + core).wait_recv()
            handed(i, d).start()

    def finish_weights(i):
        for d in range(chips):
            arrival(i, ((chip + d) % chips) * 2 + 1 - core).wait_recv()
        pltpu.make_async_copy(weights[i][0], weights[i][1].at[me], own_sem.at[i]).wait()

    def weight_slab(ref, lanes):
        if depth % 16 == 0:
            return ref[:, :, lanes].reshape(channels, SLAB)
        return jnp.concatenate([ref[s, :, lanes].astype(F32) for s in range(count)]).astype(BF16)

    def go(f, b, n, origin):
        return pltpu.make_async_remote_copy(
            src_ref=normed.at[f, b * count + n],
            dst_ref=xin.at[f, b, origin],
            send_sem=go_send.at[f, b, n],
            recv_sem=go_recv.at[f, b, origin],
            device_id={"frame": n},
            device_id_type=MESH,
        )

    def send_back(b, g, n, origin):
        lanes = pl.ds(BACK[g][2], BACK[g][3])
        return pltpu.make_async_remote_copy(
            src_ref=tmix.at[:, b, n, :, lanes],
            dst_ref=back.at[:, b * count + origin, :, lanes],
            send_sem=back_send.at[b, g, n],
            recv_sem=back_recv.at[b, g, origin],
            device_id={"frame": n},
            device_id_type=MESH,
        )

    def others(step):
        def body(d, c):
            step((me + d) % count)
            return c

        lax.fori_loop(1, count, body, 0)

    rows_t = frames_here * count * 8
    blocks = frames_here * count // BLOCK
    band = 8 * BLOCK // frames_here
    key_id = lax.broadcasted_iota(jnp.int32, (1, rows_t), 1)
    key_block = ((key_id // 8) % count) * frames_here // BLOCK
    row_id = lax.broadcasted_iota(jnp.int32, (band, rows_t), 0)
    col_id = lax.broadcasted_iota(jnp.int32, (band, rows_t), 1)
    same = (row_id % 8) == (col_id % 8)
    for i in range(blocks):
        allowed = jnp.zeros((1, rows_t), jnp.int32)
        for j in range(blocks):
            allowed = jnp.where(key_block == j, mask_ref[i, j], allowed)
        plane = jnp.where(same & (allowed == 1), 0.0, -1e30).astype(F32)
        for f in range(frames_here):
            start = f * count * 8 + i * band
            bias[start : start + band, :] = plane

    def put_tiles(dst, first, rows, lanes):
        for w, tile in enumerate(to_tiles(rows)):
            dst[first + w, :, lanes] = tile.astype(BF16)

    def spatial_step(f, g):
        lanes = pl.ds(GROUPS[g][0], GROUPS[g][1])
        put_tiles(tiles_q, 0, q_ref[f, :, :, lanes], lanes)
        put_tiles(tiles_k, tiles_wide, k_ref[f, :, :, lanes], lanes)
        put_tiles(tiles_v, tiles_wide, v_ref[f, :, :, lanes], lanes)

        @pl.when(has_up)
        def _():
            halo(0, f, g, 0).wait_recv()
            put_tiles(tiles_k, 0, halo_k[0, f, :, :, lanes], lanes)
            halo(0, f, g, 1).wait_recv()
            put_tiles(tiles_v, 0, halo_v[0, f, :, :, lanes], lanes)

        @pl.when(has_down)
        def _():
            halo(1, f, g, 0).wait_recv()
            put_tiles(tiles_k, 2 * tiles_wide, halo_k[1, f, :, :, lanes], lanes)
            halo(1, f, g, 1).wait_recv()
            put_tiles(tiles_v, 2 * tiles_wide, halo_v[1, f, :, :, lanes], lanes)

        def pair_body(p, c):
            window = pl.ds(pl.multiple_of(p * 128, 128), 256)
            first, second = pair_masks(p, head, BF16)
            first32, second32 = pair_masks(p, head, F32)
            for w in range(tiles_wide):
                picks = [
                    jnp.clip(list_ref[w, s] - (tile_row - 1) * tiles_wide, 0, 3 * tiles_wide - 1)
                    for s in range(SLOTS)
                ]
                query = tiles_q[w, :, window]
                query = jnp.concatenate([query * first, query * second], axis=0)
                keys = jnp.concatenate([tiles_k[i, :, window] for i in picks], axis=0)
                values = jnp.concatenate([tiles_v[i, :, window] for i in picks], axis=0)
                s = lax.dot_general(
                    query, keys, (((1,), (1,)), ((), ())), preferred_element_type=F32
                )
                peak = jnp.max(s, axis=-1, keepdims=True)
                e = jnp.exp2((s - peak) * scale)
                e = e * (1.0 / jnp.sum(e, axis=-1, keepdims=True))
                o = jnp.dot(e.astype(BF16), values, preferred_element_type=F32)
                o = o[:64] * first32 + o[64:] * second32
                heads[w, :, window] += o.astype(BF16)
            return c

        lax.fori_loop(GROUPS[g][2], GROUPS[g][3], pair_body, 0)

    def project_out(f, k0, k1):
        x = heads[:, :, k0:k1].reshape(spots, k1 - k0)
        for n in range(channels // SLAB):
            lanes = pl.ds(n * SLAB, SLAB)
            y = jnp.dot(x, weight_slab(wo, lanes)[k0:k1], preferred_element_type=F32)
            if k0 == 0:
                for w, tile in enumerate(to_tiles(res_ref[f, :, :, lanes])):
                    mix[w, :, lanes] = tile + y[w * 64 : (w + 1) * 64]
            else:
                mix[:, :, lanes] += y.reshape(tiles_wide, 64, SLAB)

    def normalize(f):
        gain = 1.0 + scale_ref[...].reshape(1, channels)
        offset = shift_ref[...].reshape(1, channels)

        def norm_body(w, c):
            x = mix[w].astype(BF16).astype(F32) + pos_ref[f : f + 1, :]
            centred = x - jnp.mean(x, axis=-1, keepdims=True)
            spread = jnp.mean(centred * centred, axis=-1, keepdims=True)
            y = centred * lax.rsqrt(spread + EPS) * gain + offset
            normed[f, pl.ds(w * 4, 4)] = y.astype(BF16).reshape(4, 16, channels)
            return c

        share = tiles_wide // parts
        for b in range(parts):
            lax.fori_loop(b * share, (b + 1) * share, norm_body, 0)
            others(lambda n: go(f, b, n, me).start())
            xin[f, b, me] = normed[f, b * count + me]

    for copy in inputs:
        copy.wait()
    for f in range(frames_here):
        heads[...] = jnp.zeros_like(heads)
        for g in range(len(GROUPS)):
            spatial_step(f, g)
            if f == 0 and g == 0:
                hand_on(0)
            if f == 0 and g == 2:
                finish_weights(0)
            if f == 1 and g == 0:
                hand_on(1)
            if f == 1 and g == 1:
                project_out(f, 0, 768)
        if f == 0:
            project_out(f, 0, channels)
        else:
            project_out(f, 768, channels)
        normalize(f)

    tmix[...] = jnp.zeros_like(tmix)
    finish_weights(1)

    def project_in(b):
        for f in range(frames_here):
            others(lambda n: go(f, b, n, n).wait_recv())
        x = xin[:, b].reshape(2 * rows_t, channels)

        def slab_body(n, c):
            lanes = pl.ds(pl.multiple_of(n * SLAB, 128), SLAB)
            y = jnp.dot(x, weight_slab(wq, lanes), preferred_element_type=F32)
            y = y.reshape(frames_here, count, 2, 8, SLAB)
            for half in range(2):
                z = y[:, :, half].reshape(frames_here, count * 8, SLAB)
                proj[:, b, half, :, lanes] = z.astype(BF16)
            return c

        lax.fori_loop(0, 3 * channels // SLAB, slab_body, 0)

    def temporal_pair(b, p, c):
        start = pl.multiple_of(p * 128, 128)
        window = pl.ds(start, 256)
        masks = pair_masks(p, head, BF16)
        masks32 = pair_masks(p, head, F32)
        found = []
        for half in range(2):
            query = proj[:, b, half, :, window].reshape(rows_t, 256)
            keys = proj[:, b, half, :, pl.ds(start + channels, 256)].reshape(rows_t, 256)
            values = proj[:, b, half, :, pl.ds(start + 2 * channels, 256)]
            values = values.reshape(rows_t, 256)
            query = jnp.concatenate([query * masks[0], query * masks[1]], axis=0)
            s = lax.dot_general(
                query, keys, (((1,), (1,)), ((), ())), preferred_element_type=F32
            )
            s = s.reshape(2, rows_t, rows_t) + bias[...]
            peak = jnp.max(s, axis=-1, keepdims=True)
            e = jnp.exp2((s - peak) * scale)
            e = e * (1.0 / jnp.sum(e, axis=-1, keepdims=True))
            e = e.astype(BF16).reshape(2 * rows_t, rows_t)
            o = jnp.dot(e, values, preferred_element_type=F32)
            o = o[:rows_t] * masks32[0] + o[rows_t:] * masks32[1]
            found.append(o.reshape(frames_here, count, 8, 256))
        both = jnp.stack(found, axis=2).reshape(frames_here, count, 16, 256)
        tmix[:, b, :, :, window] += both.astype(BF16)
        return c

    for b in range(parts):
        project_in(b)
        for g, (p0, p1, lane0, width) in enumerate(BACK):
            lax.fori_loop(p0, p1, functools.partial(temporal_pair, b), 0)
            others(lambda n: send_back(b, g, n, me).start())
            lanes = pl.ds(lane0, width)
            back[:, b * count + me, :, lanes] = tmix[:, b, me, :, lanes]

    share = tiles_wide // parts * TILE
    for b in range(parts):
        for g, (p0, p1, lane0, width) in enumerate(BACK):
            others(lambda n: send_back(b, g, n, n).wait_recv())
            lanes = pl.ds(lane0, width)
            for f in range(frames_here):
                for i in range(height // 2):
                    got = [
                        back[f, w * (height // 2) + i, :, lanes].astype(F32)
                        for w in range(b * tiles_wide // parts, (b + 1) * tiles_wide // parts)
                    ]
                    for half in range(2):
                        out_ref[f, 2 * i + half, b * share : (b + 1) * share, lanes] = (
                            jnp.concatenate(
                                [x[half * 8 : half * 8 + 8] for x in got], axis=0
                            ).astype(BF16)
                        )

    each_halo(lambda copy: copy.wait_send())
    for i in range(2):
        for d in range(1, chips):
            direct(i, d).wait_send()
            handed(i, d).wait_send()
        own_to_sibling(i).wait_send()
    for b in range(parts):
        for f in range(frames_here):
            others(lambda n: go(f, b, n, me).wait_send())
        for g in range(len(BACK)):
            others(lambda n: send_back(b, g, n, me).wait_send())


def local(
    count,
    rows_axis,
    spatial_q,
    spatial_k,
    spatial_v,
    residual,
    neighbour_list,
    block_mask,
    out_weight,
    qkv_weight,
    pos_embed,
    mod_shift,
    mod_scale,
):
    frames_here, height, breadth, channels = spatial_q.shape
    tiles_wide = breadth // TILE
    spots = height * breadth
    parts = spots // count // 16
    chips = count // 2
    depth = out_weight.shape[0]
    groups = len(GROUPS)
    rows_t = frames_here * count * 8
    vmem = pl.BlockSpec(memory_space=pltpu.VMEM)
    smem = pl.BlockSpec(memory_space=pltpu.SMEM)
    hbm = pl.BlockSpec(memory_space=pl.ANY)
    dma = pltpu.SemaphoreType.DMA
    return pl.pallas_call(
        functools.partial(kernel, count, rows_axis),
        out_shape=jax.ShapeDtypeStruct(spatial_q.shape, BF16),
        in_specs=[hbm, hbm, hbm, hbm, smem, smem, hbm, hbm, vmem, vmem, vmem],
        out_specs=vmem,
        scratch_shapes=[
            pltpu.VMEM((frames_here, height, breadth, channels), BF16),
            pltpu.VMEM((frames_here, height, breadth, channels), BF16),
            pltpu.VMEM((frames_here, height, breadth, channels), BF16),
            pltpu.VMEM((frames_here, height, breadth, channels), BF16),
            pltpu.VMEM((2, frames_here, height, breadth, channels), BF16),
            pltpu.VMEM((2, frames_here, height, breadth, channels), BF16),
            pltpu.VMEM((tiles_wide, 64, channels), BF16),
            pltpu.VMEM((3 * tiles_wide, 64, channels), BF16),
            pltpu.VMEM((3 * tiles_wide, 64, channels), BF16),
            pltpu.VMEM((count, depth, channels), BF16),
            pltpu.VMEM((count, depth, 3 * channels), BF16),
            pltpu.VMEM((tiles_wide, 64, channels), BF16),
            pltpu.VMEM((tiles_wide, 64, channels), F32),
            pltpu.VMEM((frames_here, spots // 16, 16, channels), BF16),
            pltpu.VMEM((frames_here, parts, count, 16, channels), BF16),
            pltpu.VMEM((frames_here, parts, 2, count * 8, 3 * channels), BF16),
            pltpu.VMEM((frames_here, parts, count, 16, channels), BF16),
            pltpu.VMEM((frames_here, spots // 16, 16, channels), BF16),
            pltpu.VMEM((rows_t, rows_t), F32),
            dma((2, frames_here, groups, 2)),
            dma((2, frames_here, groups, 2)),
            dma((2,)),
            dma((4,)),
            dma((2, chips)),
            dma((2, chips)),
            dma((2, count)),
            dma((frames_here, parts, count)),
            dma((frames_here, parts, count)),
            dma((parts, len(BACK), count)),
            dma((parts, len(BACK), count)),
        ],
        compiler_params=pltpu.CompilerParams(
            collective_id=0, has_side_effects=True, vmem_limit_bytes=60 * 2**20
        ),
    )(
        spatial_q,
        spatial_k,
        spatial_v,
        residual,
        neighbour_list,
        block_mask,
        out_weight,
        qkv_weight,
        pos_embed,
        mod_shift,
        mod_scale,
    )


def solution(mesh):
    return jax.shard_map(
        functools.partial(local, mesh.shape["frame"], mesh.shape["row"]),
        mesh=mesh,
        in_specs=(
            P("frame", "row", None, None),
            P("frame", "row", None, None),
            P("frame", "row", None, None),
            P("frame", "row", None, None),
            P("row", None),
            P(),
            P("frame", None),
            P("frame", None),
            P("frame", None),
            P(),
            P(),
        ),
        out_specs=P("frame", "row", None, None),
        check_vma=False,
    )
```

```python
import functools
import math

import jax
import jax.numpy as jnp
from jax import lax
from jax.experimental import pallas as pl
from jax.experimental.pallas import tpu as pltpu
from jax.sharding import PartitionSpec as P

HEADS = 16
TILE = 8
SLOTS = 6
ROWS = 32
BLOCK = 4
EPS = 1e-06
MESH = pl.DeviceIdType.MESH
F32 = jnp.float32
BF16 = jnp.bfloat16

GROUPS = ((0, 512, 0, 3), (512, 384, 3, 6), (896, 256, 6, 8))
BACK = ((0, 3, 0, 384), (3, 6, 384, 384), (6, 8, 768, 384))
SLAB = 384


def pair_masks(pair, head, dtype):
    lane = lax.broadcasted_iota(jnp.int32, (1, 256), 1) - 2 * (head - 64) * pair
    first = ((lane >= 0) & (lane < head)).astype(F32)
    second = ((lane >= head) & (lane < 2 * head)).astype(F32)
    return first.astype(dtype), second.astype(dtype)


def to_tiles(rows):
    wide = rows.astype(F32)
    return [
        wide[:, w * TILE : (w + 1) * TILE, :].reshape(TILE * TILE, wide.shape[-1])
        for w in range(rows.shape[1] // TILE)
    ]


def kernel(
    count,
    rows_axis,
    q_hbm,
    k_hbm,
    v_hbm,
    res_hbm,
    list_ref,
    mask_ref,
    wo_hbm,
    wq_hbm,
    pos_ref,
    shift_ref,
    scale_ref,
    out_ref,
    q_ref,
    k_ref,
    v_ref,
    res_ref,
    halo_k,
    halo_v,
    tiles_q,
    tiles_k,
    tiles_v,
    wo,
    wq,
    heads,
    mix,
    normed,
    xin,
    proj,
    tmix,
    back,
    bias,
    halo_send,
    halo_recv,
    own_sem,
    in_sem,
    direct_send,
    pass_send,
    w_recv,
    go_send,
    go_recv,
    back_send,
    back_recv,
):
    frames_here, height, breadth, channels = q_hbm.shape
    head = channels // HEADS
    spots = height * breadth
    piece = spots // count
    parts = piece // 16
    tiles_wide = breadth // TILE
    tile_rows = ROWS // TILE
    depth = wo_hbm.shape[0]
    chips = count // 2
    me = lax.axis_index("frame")
    row = lax.axis_index("row")
    core = me % 2
    chip = me // 2
    sibling = me + 1 - 2 * core
    up = (row + rows_axis - 1) % rows_axis
    down = (row + 1) % rows_axis
    tile_row = (row + 1) % tile_rows
    has_up = tile_row > 0
    has_down = tile_row < tile_rows - 1
    scale = math.log2(math.e) / math.sqrt(head)

    barrier = pltpu.get_barrier_semaphore()

    def greet(d, c):
        pl.semaphore_signal(
            barrier, inc=1, device_id={"frame": (me + d) % count}, device_id_type=MESH
        )
        return c

    lax.fori_loop(1, count, greet, 0)

    @pl.when(has_up)
    def _():
        pl.semaphore_signal(barrier, inc=1, device_id={"row": up}, device_id_type=MESH)

    @pl.when(has_down)
    def _():
        pl.semaphore_signal(barrier, inc=1, device_id={"row": down}, device_id_type=MESH)

    peers = count - 1 + (tile_row + tile_rows - 1) // tile_rows
    peers = peers + (2 * tile_rows - 2 - tile_row) // tile_rows
    pl.semaphore_wait(barrier, peers)

    def halo(slot, f, g, t):
        lanes = pl.ds(GROUPS[g][0], GROUPS[g][1])
        source = (k_hbm, v_hbm)[t]
        target = (halo_k, halo_v)[t]
        return pltpu.make_async_remote_copy(
            src_ref=source.at[f, :, :, lanes],
            dst_ref=target.at[slot, f, :, :, lanes],
            send_sem=halo_send.at[slot, f, g, t],
            recv_sem=halo_recv.at[slot, f, g, t],
            device_id={"row": down if slot == 0 else up},
            device_id_type=MESH,
        )

    halos = [
        (f, g, t) for f in range(frames_here) for g in range(len(GROUPS)) for t in range(2)
    ]

    def each_halo(step, chosen=halos):
        for f, g, t in chosen:

            @pl.when(has_up)
            def _():
                step(halo(1, f, g, t))

            @pl.when(has_down)
            def _():
                step(halo(0, f, g, t))

    def start_halos(f, g):
        each_halo(lambda copy: copy.start(), [(f, g, 0), (f, g, 1)])

    inputs = [
        pltpu.make_async_copy(source, target, in_sem.at[i])
        for i, (source, target) in enumerate(
            ((q_hbm, q_ref), (k_hbm, k_ref), (v_hbm, v_ref), (res_hbm, res_ref))
        )
    ]

    pieces = 1 + wq_hbm.shape[1] // channels

    def here(i):
        return wo_hbm if i == 0 else wq_hbm.at[:, pl.ds((i - 1) * channels, channels)]

    def slot(i, shard):
        if i == 0:
            return wo.at[shard]
        return wq.at[shard, :, pl.ds((i - 1) * channels, channels)]

    def weight_copy(i, source, shard, send_sem, other):
        return pltpu.make_async_remote_copy(
            src_ref=source,
            dst_ref=slot(i, shard),
            send_sem=send_sem,
            recv_sem=w_recv.at[i, shard],
            device_id={"frame": other},
            device_id_type=MESH,
        )

    def peer(d):
        return ((chip + d) % chips) * 2 + core

    def direct(i, d):
        return weight_copy(i, here(i), me, direct_send.at[i, d], peer(d))

    def handed(i, d):
        return weight_copy(i, slot(i, peer(d)), peer(d), pass_send.at[i, d], sibling)

    def own_to_sibling(i):
        return weight_copy(i, here(i), me, pass_send.at[i, 0], sibling)

    def arrival(i, shard):
        return weight_copy(i, here(i), shard, pass_send.at[i, 0], sibling)

    def own(i):
        return pltpu.make_async_copy(here(i), slot(i, me), own_sem.at[i])

    def start_weights(i):
        for d in range(1, chips):
            direct(i, d).start()
        own_to_sibling(i).start()
        own(i).start()

    def hand_on(i):
        for d in range(1, chips):
            arrival(i, peer(d)).wait_recv()
            handed(i, d).start()

    def finish_weights(i):
        for d in range(chips):
            arrival(i, peer(d) + 1 - 2 * core).wait_recv()
        own(i).wait()

    steps = [(f, g) for f in range(frames_here) for g in range(len(GROUPS))]
    for i, (f, g) in enumerate(steps):
        if i < pieces:
            start_weights(i)
        start_halos(f, g)
        if i == 0:
            for copy in inputs:
                copy.start()

    def weight_slab(ref, lanes):
        if depth % 16 == 0:
            return ref[:, :, lanes].reshape(channels, SLAB)
        return jnp.concatenate([ref[s, :, lanes].astype(F32) for s in range(count)]).astype(BF16)

    def go(f, b, n, origin):
        return pltpu.make_async_remote_copy(
            src_ref=normed.at[f, b * count + n],
            dst_ref=xin.at[f, b, origin],
            send_sem=go_send.at[f, b, n],
            recv_sem=go_recv.at[f, b, origin],
            device_id={"frame": n},
            device_id_type=MESH,
        )

    def send_back(b, g, n, origin):
        lanes = pl.ds(BACK[g][2], BACK[g][3])
        return pltpu.make_async_remote_copy(
            src_ref=tmix.at[:, b, n, :, lanes],
            dst_ref=back.at[:, b * count + origin, :, lanes],
            send_sem=back_send.at[b, g, n],
            recv_sem=back_recv.at[b, g, origin],
            device_id={"frame": n},
            device_id_type=MESH,
        )

    def others(step):
        def body(d, c):
            step((me + d) % count)
            return c

        lax.fori_loop(1, count, body, 0)

    rows_t = frames_here * count * 8
    blocks = frames_here * count // BLOCK
    band = 8 * BLOCK // frames_here
    key_id = lax.broadcasted_iota(jnp.int32, (1, rows_t), 1)
    key_block = ((key_id // 8) % count) * frames_here // BLOCK
    row_id = lax.broadcasted_iota(jnp.int32, (band, rows_t), 0)
    col_id = lax.broadcasted_iota(jnp.int32, (band, rows_t), 1)
    same = (row_id % 8) == (col_id % 8)
    for i in range(blocks):
        allowed = jnp.zeros((1, rows_t), jnp.int32)
        for j in range(blocks):
            allowed = jnp.where(key_block == j, mask_ref[i, j], allowed)
        plane = jnp.where(same & (allowed == 1), 0.0, -1e30).astype(F32)
        for f in range(frames_here):
            start = f * count * 8 + i * band
            bias[start : start + band, :] = plane

    def put_tiles(dst, first, rows, lanes):
        for w, tile in enumerate(to_tiles(rows)):
            dst[first + w, :, lanes] = tile.astype(BF16)

    def spatial_step(f, g):
        lanes = pl.ds(GROUPS[g][0], GROUPS[g][1])
        put_tiles(tiles_q, 0, q_ref[f, :, :, lanes], lanes)
        put_tiles(tiles_k, tiles_wide, k_ref[f, :, :, lanes], lanes)
        put_tiles(tiles_v, tiles_wide, v_ref[f, :, :, lanes], lanes)

        @pl.when(has_up)
        def _():
            halo(0, f, g, 0).wait_recv()
            put_tiles(tiles_k, 0, halo_k[0, f, :, :, lanes], lanes)
            halo(0, f, g, 1).wait_recv()
            put_tiles(tiles_v, 0, halo_v[0, f, :, :, lanes], lanes)

        @pl.when(has_down)
        def _():
            halo(1, f, g, 0).wait_recv()
            put_tiles(tiles_k, 2 * tiles_wide, halo_k[1, f, :, :, lanes], lanes)
            halo(1, f, g, 1).wait_recv()
            put_tiles(tiles_v, 2 * tiles_wide, halo_v[1, f, :, :, lanes], lanes)

        def pair_body(p, c):
            window = pl.ds(pl.multiple_of(p * 128, 128), 256)
            first, second = pair_masks(p, head, BF16)
            first32, second32 = pair_masks(p, head, F32)
            for w in range(tiles_wide):
                picks = [
                    jnp.clip(list_ref[w, s] - (tile_row - 1) * tiles_wide, 0, 3 * tiles_wide - 1)
                    for s in range(SLOTS)
                ]
                query = tiles_q[w, :, window]
                query = jnp.concatenate([query * first, query * second], axis=0)
                keys = jnp.concatenate([tiles_k[i, :, window] for i in picks], axis=0)
                values = jnp.concatenate([tiles_v[i, :, window] for i in picks], axis=0)
                s = lax.dot_general(
                    query, keys, (((1,), (1,)), ((), ())), preferred_element_type=F32
                )
                peak = jnp.max(s, axis=-1, keepdims=True)
                e = jnp.exp2((s - peak) * scale)
                e = e * (1.0 / jnp.sum(e, axis=-1, keepdims=True))
                o = jnp.dot(e.astype(BF16), values, preferred_element_type=F32)
                o = o[:64] * first32 + o[64:] * second32
                heads[w, :, window] += o.astype(BF16)
            return c

        lax.fori_loop(GROUPS[g][2], GROUPS[g][3], pair_body, 0)

    def project_out(f, k0, k1):
        x = heads[:, :, k0:k1].reshape(spots, k1 - k0)
        for n in range(channels // SLAB):
            lanes = pl.ds(n * SLAB, SLAB)
            y = jnp.dot(x, weight_slab(wo, lanes)[k0:k1], preferred_element_type=F32)
            if k0 == 0:
                for w, tile in enumerate(to_tiles(res_ref[f, :, :, lanes])):
                    mix[w, :, lanes] = tile + y[w * 64 : (w + 1) * 64]
            else:
                mix[:, :, lanes] += y.reshape(tiles_wide, 64, SLAB)

    def normalize(f):
        gain = 1.0 + scale_ref[...].reshape(1, channels)
        offset = shift_ref[...].reshape(1, channels)

        def norm_body(w, c):
            x = mix[w].astype(BF16).astype(F32) + pos_ref[f : f + 1, :]
            centred = x - jnp.mean(x, axis=-1, keepdims=True)
            spread = jnp.mean(centred * centred, axis=-1, keepdims=True)
            y = centred * lax.rsqrt(spread + EPS) * gain + offset
            normed[f, pl.ds(w * 4, 4)] = y.astype(BF16).reshape(4, 16, channels)
            return c

        share = tiles_wide // parts
        for b in range(parts):
            lax.fori_loop(b * share, (b + 1) * share, norm_body, 0)
            others(lambda n: go(f, b, n, me).start())
            xin[f, b, me] = normed[f, b * count + me]

    for copy in inputs:
        copy.wait()
    for f in range(frames_here):
        heads[...] = jnp.zeros_like(heads)
        for g in range(len(GROUPS)):
            spatial_step(f, g)
            step = f * len(GROUPS) + g
            if step < pieces:
                hand_on(step)
            if f == 0 and g == 2:
                finish_weights(0)
            if f == 1 and g == 1:
                project_out(f, 0, 768)
        if f == 0:
            project_out(f, 0, channels)
        else:
            project_out(f, 768, channels)
        normalize(f)

    tmix[...] = jnp.zeros_like(tmix)
    for i in range(1, pieces):
        finish_weights(i)

    def project_in(b):
        for f in range(frames_here):
            others(lambda n: go(f, b, n, n).wait_recv())
        x = xin[:, b].reshape(2 * rows_t, channels)

        def slab_body(n, c):
            lanes = pl.ds(pl.multiple_of(n * SLAB, 128), SLAB)
            y = jnp.dot(x, weight_slab(wq, lanes), preferred_element_type=F32)
            y = y.reshape(frames_here, count, 2, 8, SLAB)
            for half in range(2):
                z = y[:, :, half].reshape(frames_here, count * 8, SLAB)
                proj[:, b, half, :, lanes] = z.astype(BF16)
            return c

        lax.fori_loop(0, 3 * channels // SLAB, slab_body, 0)

    def temporal_pair(b, p, c):
        start = pl.multiple_of(p * 128, 128)
        window = pl.ds(start, 256)
        masks = pair_masks(p, head, BF16)
        masks32 = pair_masks(p, head, F32)
        found = []
        for half in range(2):
            query = proj[:, b, half, :, window].reshape(rows_t, 256)
            keys = proj[:, b, half, :, pl.ds(start + channels, 256)].reshape(rows_t, 256)
            values = proj[:, b, half, :, pl.ds(start + 2 * channels, 256)]
            values = values.reshape(rows_t, 256)
            query = jnp.concatenate([query * masks[0], query * masks[1]], axis=0)
            s = lax.dot_general(
                query, keys, (((1,), (1,)), ((), ())), preferred_element_type=F32
            )
            s = s.reshape(2, rows_t, rows_t) + bias[...]
            peak = jnp.max(s, axis=-1, keepdims=True)
            e = jnp.exp2((s - peak) * scale)
            e = e * (1.0 / jnp.sum(e, axis=-1, keepdims=True))
            e = e.astype(BF16).reshape(2 * rows_t, rows_t)
            o = jnp.dot(e, values, preferred_element_type=F32)
            o = o[:rows_t] * masks32[0] + o[rows_t:] * masks32[1]
            found.append(o.reshape(frames_here, count, 8, 256))
        both = jnp.stack(found, axis=2).reshape(frames_here, count, 16, 256)
        tmix[:, b, :, :, window] += both.astype(BF16)
        return c

    for b in range(parts):
        project_in(b)
        for g, (p0, p1, lane0, width) in enumerate(BACK):
            lax.fori_loop(p0, p1, functools.partial(temporal_pair, b), 0)
            others(lambda n: send_back(b, g, n, me).start())
            lanes = pl.ds(lane0, width)
            back[:, b * count + me, :, lanes] = tmix[:, b, me, :, lanes]

    share = tiles_wide // parts * TILE
    for b in range(parts):
        for g, (p0, p1, lane0, width) in enumerate(BACK):
            others(lambda n: send_back(b, g, n, n).wait_recv())
            lanes = pl.ds(lane0, width)
            for f in range(frames_here):
                for i in range(height // 2):
                    got = [
                        back[f, w * (height // 2) + i, :, lanes].astype(F32)
                        for w in range(b * tiles_wide // parts, (b + 1) * tiles_wide // parts)
                    ]
                    for half in range(2):
                        out_ref[f, 2 * i + half, b * share : (b + 1) * share, lanes] = (
                            jnp.concatenate(
                                [x[half * 8 : half * 8 + 8] for x in got], axis=0
                            ).astype(BF16)
                        )

    each_halo(lambda copy: copy.wait_send())
    for i in range(pieces):
        for d in range(1, chips):
            direct(i, d).wait_send()
            handed(i, d).wait_send()
        own_to_sibling(i).wait_send()
    for b in range(parts):
        for f in range(frames_here):
            others(lambda n: go(f, b, n, me).wait_send())
        for g in range(len(BACK)):
            others(lambda n: send_back(b, g, n, me).wait_send())


def local(
    count,
    rows_axis,
    spatial_q,
    spatial_k,
    spatial_v,
    residual,
    neighbour_list,
    block_mask,
    out_weight,
    qkv_weight,
    pos_embed,
    mod_shift,
    mod_scale,
):
    frames_here, height, breadth, channels = spatial_q.shape
    tiles_wide = breadth // TILE
    spots = height * breadth
    parts = spots // count // 16
    chips = count // 2
    depth = out_weight.shape[0]
    groups = len(GROUPS)
    rows_t = frames_here * count * 8
    vmem = pl.BlockSpec(memory_space=pltpu.VMEM)
    smem = pl.BlockSpec(memory_space=pltpu.SMEM)
    hbm = pl.BlockSpec(memory_space=pl.ANY)
    dma = pltpu.SemaphoreType.DMA
    return pl.pallas_call(
        functools.partial(kernel, count, rows_axis),
        out_shape=jax.ShapeDtypeStruct(spatial_q.shape, BF16),
        in_specs=[hbm, hbm, hbm, hbm, smem, smem, hbm, hbm, vmem, vmem, vmem],
        out_specs=vmem,
        scratch_shapes=[
            pltpu.VMEM((frames_here, height, breadth, channels), BF16),
            pltpu.VMEM((frames_here, height, breadth, channels), BF16),
            pltpu.VMEM((frames_here, height, breadth, channels), BF16),
            pltpu.VMEM((frames_here, height, breadth, channels), BF16),
            pltpu.VMEM((2, frames_here, height, breadth, channels), BF16),
            pltpu.VMEM((2, frames_here, height, breadth, channels), BF16),
            pltpu.VMEM((tiles_wide, 64, channels), BF16),
            pltpu.VMEM((3 * tiles_wide, 64, channels), BF16),
            pltpu.VMEM((3 * tiles_wide, 64, channels), BF16),
            pltpu.VMEM((count, depth, channels), BF16),
            pltpu.VMEM((count, depth, 3 * channels), BF16),
            pltpu.VMEM((tiles_wide, 64, channels), BF16),
            pltpu.VMEM((tiles_wide, 64, channels), F32),
            pltpu.VMEM((frames_here, spots // 16, 16, channels), BF16),
            pltpu.VMEM((frames_here, parts, count, 16, channels), BF16),
            pltpu.VMEM((frames_here, parts, 2, count * 8, 3 * channels), BF16),
            pltpu.VMEM((frames_here, parts, count, 16, channels), BF16),
            pltpu.VMEM((frames_here, spots // 16, 16, channels), BF16),
            pltpu.VMEM((rows_t, rows_t), F32),
            dma((2, frames_here, groups, 2)),
            dma((2, frames_here, groups, 2)),
            dma((4,)),
            dma((4,)),
            dma((4, chips)),
            dma((4, chips)),
            dma((4, count)),
            dma((frames_here, parts, count)),
            dma((frames_here, parts, count)),
            dma((parts, len(BACK), count)),
            dma((parts, len(BACK), count)),
        ],
        compiler_params=pltpu.CompilerParams(
            collective_id=0, has_side_effects=True, vmem_limit_bytes=60 * 2**20
        ),
    )(
        spatial_q,
        spatial_k,
        spatial_v,
        residual,
        neighbour_list,
        block_mask,
        out_weight,
        qkv_weight,
        pos_embed,
        mod_shift,
        mod_scale,
    )


def solution(mesh):
    return jax.shard_map(
        functools.partial(local, mesh.shape["frame"], mesh.shape["row"]),
        mesh=mesh,
        in_specs=(
            P("frame", "row", None, None),
            P("frame", "row", None, None),
            P("frame", "row", None, None),
            P("frame", "row", None, None),
            P("row", None),
            P(),
            P("frame", None),
            P("frame", None),
            P("frame", None),
            P(),
            P(),
        ),
        out_specs=P("frame", "row", None, None),
        check_vma=False,
    )
```

```python
import functools
import math

import jax
import jax.numpy as jnp
from jax import lax
from jax.experimental import pallas as pl
from jax.experimental.pallas import tpu as pltpu
from jax.sharding import PartitionSpec as P

HEADS = 16
TILE = 8
SLOTS = 6
ROWS = 32
BLOCK = 4
EPS = 1e-06
MESH = pl.DeviceIdType.MESH
F32 = jnp.float32
BF16 = jnp.bfloat16

GROUPS = ((0, 512, 0, 3), (512, 384, 3, 6), (896, 256, 6, 8))
BACK = ((0, 3, 0, 384), (3, 6, 384, 384), (6, 8, 768, 384))
SLAB = 384


def pair_masks(pair, head, dtype):
    lane = lax.broadcasted_iota(jnp.int32, (1, 256), 1) - 2 * (head - 64) * pair
    first = ((lane >= 0) & (lane < head)).astype(F32)
    second = ((lane >= head) & (lane < 2 * head)).astype(F32)
    return first.astype(dtype), second.astype(dtype)


def to_tiles(rows):
    wide = rows.astype(F32)
    return [
        wide[:, w * TILE : (w + 1) * TILE, :].reshape(TILE * TILE, wide.shape[-1])
        for w in range(rows.shape[1] // TILE)
    ]


def kernel(
    count,
    rows_axis,
    q_ref,
    k_ref,
    v_ref,
    res_ref,
    list_ref,
    mask_ref,
    wo_hbm,
    wq_hbm,
    pos_ref,
    shift_ref,
    scale_ref,
    out_ref,
    halo_k,
    halo_v,
    tiles_q,
    tiles_k,
    tiles_v,
    wo,
    wq,
    heads,
    mix,
    normed,
    xin,
    proj,
    tmix,
    back,
    bias,
    halo_send,
    halo_recv,
    own_sem,
    direct_send,
    pass_send,
    w_recv,
    go_send,
    go_recv,
    back_send,
    back_recv,
):
    frames_here, height, breadth, channels = q_ref.shape
    head = channels // HEADS
    spots = height * breadth
    piece = spots // count
    parts = piece // 16
    tiles_wide = breadth // TILE
    tile_rows = ROWS // TILE
    depth = wo_hbm.shape[0]
    chips = count // 2
    me = lax.axis_index("frame")
    row = lax.axis_index("row")
    core = me % 2
    chip = me // 2
    sibling = me + 1 - 2 * core
    up = (row + rows_axis - 1) % rows_axis
    down = (row + 1) % rows_axis
    tile_row = (row + 1) % tile_rows
    has_up = tile_row > 0
    has_down = tile_row < tile_rows - 1
    scale = math.log2(math.e) / math.sqrt(head)

    barrier = pltpu.get_barrier_semaphore()

    def greet(d, c):
        pl.semaphore_signal(
            barrier, inc=1, device_id={"frame": (me + d) % count}, device_id_type=MESH
        )
        return c

    lax.fori_loop(1, count, greet, 0)

    @pl.when(has_up)
    def _():
        pl.semaphore_signal(barrier, inc=1, device_id={"row": up}, device_id_type=MESH)

    @pl.when(has_down)
    def _():
        pl.semaphore_signal(barrier, inc=1, device_id={"row": down}, device_id_type=MESH)

    peers = count - 1 + (tile_row + tile_rows - 1) // tile_rows
    peers = peers + (2 * tile_rows - 2 - tile_row) // tile_rows
    pl.semaphore_wait(barrier, peers)

    def halo(slot, f, g, t):
        lanes = pl.ds(GROUPS[g][0], GROUPS[g][1])
        source = (k_ref, v_ref)[t]
        target = (halo_k, halo_v)[t]
        return pltpu.make_async_remote_copy(
            src_ref=source.at[f, :, :, lanes],
            dst_ref=target.at[slot, f, :, :, lanes],
            send_sem=halo_send.at[slot, f, g, t],
            recv_sem=halo_recv.at[slot, f, g, t],
            device_id={"row": down if slot == 0 else up},
            device_id_type=MESH,
        )

    halos = [
        (f, g, t) for f in range(frames_here) for g in range(len(GROUPS)) for t in range(2)
    ]

    def each_halo(step, chosen=halos):
        for f, g, t in chosen:

            @pl.when(has_up)
            def _():
                step(halo(1, f, g, t))

            @pl.when(has_down)
            def _():
                step(halo(0, f, g, t))

    def start_halos(f, g):
        each_halo(lambda copy: copy.start(), [(f, g, 0), (f, g, 1)])

    pieces = 1 + wq_hbm.shape[1] // channels

    def here(i):
        return wo_hbm if i == 0 else wq_hbm.at[:, pl.ds((i - 1) * channels, channels)]

    def slot(i, shard):
        if i == 0:
            return wo.at[shard]
        return wq.at[shard, :, pl.ds((i - 1) * channels, channels)]

    def weight_copy(i, source, shard, send_sem, other):
        return pltpu.make_async_remote_copy(
            src_ref=source,
            dst_ref=slot(i, shard),
            send_sem=send_sem,
            recv_sem=w_recv.at[i, shard],
            device_id={"frame": other},
            device_id_type=MESH,
        )

    def peer(d):
        return ((chip + d) % chips) * 2 + core

    def direct(i, d):
        return weight_copy(i, here(i), me, direct_send.at[i, d], peer(d))

    def handed(i, d):
        return weight_copy(i, slot(i, peer(d)), peer(d), pass_send.at[i, d], sibling)

    def own_to_sibling(i):
        return weight_copy(i, here(i), me, pass_send.at[i, 0], sibling)

    def arrival(i, shard):
        return weight_copy(i, here(i), shard, pass_send.at[i, 0], sibling)

    def own(i):
        return pltpu.make_async_copy(here(i), slot(i, me), own_sem.at[i])

    def start_weights(i):
        for d in range(1, chips):
            direct(i, d).start()
        own_to_sibling(i).start()
        own(i).start()

    def hand_on(i):
        for d in range(1, chips):
            arrival(i, peer(d)).wait_recv()
            handed(i, d).start()

    def finish_weights(i):
        for d in range(chips):
            arrival(i, peer(d) + 1 - 2 * core).wait_recv()
        own(i).wait()

    steps = [(f, g) for f in range(frames_here) for g in range(len(GROUPS))]
    for i, (f, g) in enumerate(steps):
        if i < pieces:
            start_weights(i)
        start_halos(f, g)

    def weight_slab(ref, lanes):
        if depth % 16 == 0:
            return ref[:, :, lanes].reshape(channels, SLAB)
        return jnp.concatenate([ref[s, :, lanes].astype(F32) for s in range(count)]).astype(BF16)

    def go(f, b, n, origin):
        return pltpu.make_async_remote_copy(
            src_ref=normed.at[f, b * count + n],
            dst_ref=xin.at[f, b, origin],
            send_sem=go_send.at[f, b, n],
            recv_sem=go_recv.at[f, b, origin],
            device_id={"frame": n},
            device_id_type=MESH,
        )

    def send_back(b, g, n, origin):
        lanes = pl.ds(BACK[g][2], BACK[g][3])
        return pltpu.make_async_remote_copy(
            src_ref=tmix.at[:, b, n, :, lanes],
            dst_ref=back.at[:, b * count + origin, :, lanes],
            send_sem=back_send.at[b, g, n],
            recv_sem=back_recv.at[b, g, origin],
            device_id={"frame": n},
            device_id_type=MESH,
        )

    def others(step):
        def body(d, c):
            step((me + d) % count)
            return c

        lax.fori_loop(1, count, body, 0)

    rows_t = frames_here * count * 8
    blocks = frames_here * count // BLOCK
    band = 8 * BLOCK // frames_here
    key_id = lax.broadcasted_iota(jnp.int32, (1, rows_t), 1)
    key_block = ((key_id // 8) % count) * frames_here // BLOCK
    row_id = lax.broadcasted_iota(jnp.int32, (band, rows_t), 0)
    col_id = lax.broadcasted_iota(jnp.int32, (band, rows_t), 1)
    same = (row_id % 8) == (col_id % 8)
    for i in range(blocks):
        allowed = jnp.zeros((1, rows_t), jnp.int32)
        for j in range(blocks):
            allowed = jnp.where(key_block == j, mask_ref[i, j], allowed)
        plane = jnp.where(same & (allowed == 1), 0.0, -1e30).astype(F32)
        for f in range(frames_here):
            start = f * count * 8 + i * band
            bias[start : start + band, :] = plane

    def put_tiles(dst, first, rows, lanes):
        for w, tile in enumerate(to_tiles(rows)):
            dst[first + w, :, lanes] = tile.astype(BF16)

    def spatial_step(f, g):
        lanes = pl.ds(GROUPS[g][0], GROUPS[g][1])
        put_tiles(tiles_q, 0, q_ref[f, :, :, lanes], lanes)
        put_tiles(tiles_k, tiles_wide, k_ref[f, :, :, lanes], lanes)
        put_tiles(tiles_v, tiles_wide, v_ref[f, :, :, lanes], lanes)

        @pl.when(has_up)
        def _():
            halo(0, f, g, 0).wait_recv()
            put_tiles(tiles_k, 0, halo_k[0, f, :, :, lanes], lanes)
            halo(0, f, g, 1).wait_recv()
            put_tiles(tiles_v, 0, halo_v[0, f, :, :, lanes], lanes)

        @pl.when(has_down)
        def _():
            halo(1, f, g, 0).wait_recv()
            put_tiles(tiles_k, 2 * tiles_wide, halo_k[1, f, :, :, lanes], lanes)
            halo(1, f, g, 1).wait_recv()
            put_tiles(tiles_v, 2 * tiles_wide, halo_v[1, f, :, :, lanes], lanes)

        def pair_body(p, c):
            window = pl.ds(pl.multiple_of(p * 128, 128), 256)
            first, second = pair_masks(p, head, BF16)
            first32, second32 = pair_masks(p, head, F32)
            for w in range(tiles_wide):
                picks = [
                    jnp.clip(list_ref[w, s] - (tile_row - 1) * tiles_wide, 0, 3 * tiles_wide - 1)
                    for s in range(SLOTS)
                ]
                query = tiles_q[w, :, window]
                query = jnp.concatenate([query * first, query * second], axis=0)
                keys = jnp.concatenate([tiles_k[i, :, window] for i in picks], axis=0)
                values = jnp.concatenate([tiles_v[i, :, window] for i in picks], axis=0)
                s = lax.dot_general(
                    keys, query, (((1,), (1,)), ((), ())), preferred_element_type=F32
                )
                peak = jnp.max(s, axis=0, keepdims=True)
                e = jnp.exp2((s - peak) * scale)
                e = e * (1.0 / jnp.sum(e, axis=0, keepdims=True))
                o = lax.dot_general(
                    e.astype(BF16), values, (((0,), (0,)), ((), ())), preferred_element_type=F32
                )
                o = o[:64] * first32 + o[64:] * second32
                heads[w, :, window] += o.astype(BF16)
            return c

        lax.fori_loop(GROUPS[g][2], GROUPS[g][3], pair_body, 0)

    def project_out(f, k0, k1):
        x = heads[:, :, k0:k1].reshape(spots, k1 - k0)
        for n in range(channels // SLAB):
            lanes = pl.ds(n * SLAB, SLAB)
            y = jnp.dot(x, weight_slab(wo, lanes)[k0:k1], preferred_element_type=F32)
            if k0 == 0:
                for w, tile in enumerate(to_tiles(res_ref[f, :, :, lanes])):
                    mix[w, :, lanes] = tile + y[w * 64 : (w + 1) * 64]
            else:
                mix[:, :, lanes] += y.reshape(tiles_wide, 64, SLAB)

    def normalize(f):
        gain = 1.0 + scale_ref[...].reshape(1, channels)
        offset = shift_ref[...].reshape(1, channels)

        def norm_body(w, c):
            x = mix[w].astype(BF16).astype(F32) + pos_ref[f : f + 1, :]
            centred = x - jnp.mean(x, axis=-1, keepdims=True)
            spread = jnp.mean(centred * centred, axis=-1, keepdims=True)
            y = centred * lax.rsqrt(spread + EPS) * gain + offset
            normed[f, pl.ds(w * 4, 4)] = y.astype(BF16).reshape(4, 16, channels)
            return c

        share = tiles_wide // parts
        for b in range(parts):
            lax.fori_loop(b * share, (b + 1) * share, norm_body, 0)
            others(lambda n: go(f, b, n, me).start())
            xin[f, b, me] = normed[f, b * count + me]

    for f in range(frames_here):
        heads[...] = jnp.zeros_like(heads)
        for g in range(len(GROUPS)):
            spatial_step(f, g)
            step = f * len(GROUPS) + g
            if step < pieces:
                hand_on(step)
            if f == 0 and g == 2:
                finish_weights(0)
            if f == 1 and g == 1:
                project_out(f, 0, 768)
        if f == 0:
            project_out(f, 0, channels)
        else:
            project_out(f, 768, channels)
        normalize(f)

    tmix[...] = jnp.zeros_like(tmix)
    for i in range(1, pieces):
        finish_weights(i)

    def project_in(b):
        for f in range(frames_here):
            others(lambda n: go(f, b, n, n).wait_recv())
        x = xin[:, b].reshape(2 * rows_t, channels)

        def slab_body(n, c):
            lanes = pl.ds(pl.multiple_of(n * SLAB, 128), SLAB)
            y = jnp.dot(x, weight_slab(wq, lanes), preferred_element_type=F32)
            y = y.reshape(frames_here, count, 2, 8, SLAB)
            for half in range(2):
                z = y[:, :, half].reshape(frames_here, count * 8, SLAB)
                proj[:, b, half, :, lanes] = z.astype(BF16)
            return c

        lax.fori_loop(0, 3 * channels // SLAB, slab_body, 0)

    def temporal_pair(b, p, c):
        start = pl.multiple_of(p * 128, 128)
        window = pl.ds(start, 256)
        masks = pair_masks(p, head, BF16)
        masks32 = pair_masks(p, head, F32)
        found = []
        for half in range(2):
            query = proj[:, b, half, :, window].reshape(rows_t, 256)
            keys = proj[:, b, half, :, pl.ds(start + channels, 256)].reshape(rows_t, 256)
            values = proj[:, b, half, :, pl.ds(start + 2 * channels, 256)]
            values = values.reshape(rows_t, 256)
            query = jnp.concatenate([query * masks[0], query * masks[1]], axis=0)
            s = lax.dot_general(
                query, keys, (((1,), (1,)), ((), ())), preferred_element_type=F32
            )
            s = s.reshape(2, rows_t, rows_t) + bias[...]
            peak = jnp.max(s, axis=-1, keepdims=True)
            e = jnp.exp2((s - peak) * scale)
            e = e * (1.0 / jnp.sum(e, axis=-1, keepdims=True))
            e = e.astype(BF16).reshape(2 * rows_t, rows_t)
            o = jnp.dot(e, values, preferred_element_type=F32)
            o = o[:rows_t] * masks32[0] + o[rows_t:] * masks32[1]
            found.append(o.reshape(frames_here, count, 8, 256))
        both = jnp.stack(found, axis=2).reshape(frames_here, count, 16, 256)
        tmix[:, b, :, :, window] += both.astype(BF16)
        return c

    for b in range(parts):
        project_in(b)
        for g, (p0, p1, lane0, width) in enumerate(BACK):
            lax.fori_loop(p0, p1, functools.partial(temporal_pair, b), 0)
            others(lambda n: send_back(b, g, n, me).start())
            lanes = pl.ds(lane0, width)
            back[:, b * count + me, :, lanes] = tmix[:, b, me, :, lanes]

    share = tiles_wide // parts * TILE
    for b in range(parts):
        for g, (p0, p1, lane0, width) in enumerate(BACK):
            others(lambda n: send_back(b, g, n, n).wait_recv())
            lanes = pl.ds(lane0, width)
            for f in range(frames_here):
                for i in range(height // 2):
                    got = [
                        back[f, w * (height // 2) + i, :, lanes].astype(F32)
                        for w in range(b * tiles_wide // parts, (b + 1) * tiles_wide // parts)
                    ]
                    for half in range(2):
                        out_ref[f, 2 * i + half, b * share : (b + 1) * share, lanes] = (
                            jnp.concatenate(
                                [x[half * 8 : half * 8 + 8] for x in got], axis=0
                            ).astype(BF16)
                        )

    each_halo(lambda copy: copy.wait_send())
    for i in range(pieces):
        for d in range(1, chips):
            direct(i, d).wait_send()
            handed(i, d).wait_send()
        own_to_sibling(i).wait_send()
    for b in range(parts):
        for f in range(frames_here):
            others(lambda n: go(f, b, n, me).wait_send())
        for g in range(len(BACK)):
            others(lambda n: send_back(b, g, n, me).wait_send())


def local(
    count,
    rows_axis,
    spatial_q,
    spatial_k,
    spatial_v,
    residual,
    neighbour_list,
    block_mask,
    out_weight,
    qkv_weight,
    pos_embed,
    mod_shift,
    mod_scale,
):
    frames_here, height, breadth, channels = spatial_q.shape
    tiles_wide = breadth // TILE
    spots = height * breadth
    parts = spots // count // 16
    chips = count // 2
    depth = out_weight.shape[0]
    groups = len(GROUPS)
    rows_t = frames_here * count * 8
    vmem = pl.BlockSpec(memory_space=pltpu.VMEM)
    smem = pl.BlockSpec(memory_space=pltpu.SMEM)
    hbm = pl.BlockSpec(memory_space=pl.ANY)
    dma = pltpu.SemaphoreType.DMA
    return pl.pallas_call(
        functools.partial(kernel, count, rows_axis),
        out_shape=jax.ShapeDtypeStruct(spatial_q.shape, BF16),
        in_specs=[vmem, vmem, vmem, vmem, smem, smem, hbm, hbm, vmem, vmem, vmem],
        out_specs=vmem,
        scratch_shapes=[
            pltpu.VMEM((2, frames_here, height, breadth, channels), BF16),
            pltpu.VMEM((2, frames_here, height, breadth, channels), BF16),
            pltpu.VMEM((tiles_wide, 64, channels), BF16),
            pltpu.VMEM((3 * tiles_wide, 64, channels), BF16),
            pltpu.VMEM((3 * tiles_wide, 64, channels), BF16),
            pltpu.VMEM((count, depth, channels), BF16),
            pltpu.VMEM((count, depth, 3 * channels), BF16),
            pltpu.VMEM((tiles_wide, 64, channels), BF16),
            pltpu.VMEM((tiles_wide, 64, channels), F32),
            pltpu.VMEM((frames_here, spots // 16, 16, channels), BF16),
            pltpu.VMEM((frames_here, parts, count, 16, channels), BF16),
            pltpu.VMEM((frames_here, parts, 2, count * 8, 3 * channels), BF16),
            pltpu.VMEM((frames_here, parts, count, 16, channels), BF16),
            pltpu.VMEM((frames_here, spots // 16, 16, channels), BF16),
            pltpu.VMEM((rows_t, rows_t), F32),
            dma((2, frames_here, groups, 2)),
            dma((2, frames_here, groups, 2)),
            dma((4,)),
            dma((4, chips)),
            dma((4, chips)),
            dma((4, count)),
            dma((frames_here, parts, count)),
            dma((frames_here, parts, count)),
            dma((parts, len(BACK), count)),
            dma((parts, len(BACK), count)),
        ],
        compiler_params=pltpu.CompilerParams(
            collective_id=0, has_side_effects=True, vmem_limit_bytes=60 * 2**20
        ),
    )(
        spatial_q,
        spatial_k,
        spatial_v,
        residual,
        neighbour_list,
        block_mask,
        out_weight,
        qkv_weight,
        pos_embed,
        mod_shift,
        mod_scale,
    )


def solution(mesh):
    return jax.shard_map(
        functools.partial(local, mesh.shape["frame"], mesh.shape["row"]),
        mesh=mesh,
        in_specs=(
            P("frame", "row", None, None),
            P("frame", "row", None, None),
            P("frame", "row", None, None),
            P("frame", "row", None, None),
            P("row", None),
            P(),
            P("frame", None),
            P("frame", None),
            P("frame", None),
            P(),
            P(),
        ),
        out_specs=P("frame", "row", None, None),
        check_vma=False,
    )
```
